256 devices in a mesh: pair: 128 (over z, x, y), aux: 2 (over core).
Axes of the slice: x: 4, y: 4, z: 8, core: 2. Of those that a mesh axis runs over, the one named last changes fastest.
Arguments:
- half_transformed: bfloat16 [256, 128, 32, 128], P('pair', None, 'aux'), may hold values from -1.5 to 1.5
- trials: bfloat16 [256, 128, 128], P('pair'), may hold values from -0.047851562 to 0.047851562
- pair_table: int32 [8192, 2], P('pair'), may hold values from 0 to 255, as said below
- block_slot: int32 [256], replicated, may hold values from 0 to 255, as said below
- domains: int32 [256, 128], replicated, may hold values from 0 to 4591, as said below
Outputs:
- applied: float32 [256, 128, 128], P('pair')
The draws below stay inside these ranges and needn't reach their ends.
Inputs may be any that keep to these rules, and one draw needn't show every extreme that they name: `block_slot`: A permutation of the block numbers. `pair_table`: both blocks of every pair listed in rows p * 64 to (p + 1) * 64 - 1 stand, by block_slot, in rows (p - 2) * 2 to (p + 3) * 2 - 1 of the blocked arrays. A pair may repeat and may name one block twice. `domains`: the 128 orbital numbers of one row are distinct.
All inputs are finite; a program needn't handle non-finite values.
Results may differ from the reference program's by a relative error of at most 0.0022.
Values may be sent and summed in bfloat16 or wider, within the bound.
A program may use at most 64 MiB of HBM per device.

```python
import jax
import jax.numpy as jnp
from jax import lax

BS = 128
OCC_DOM = 128
NV = 128
AUX_DEV = 16
BLK_DEV = 2
PAIR_DEV = 64
REACH = 2
NBLK = 256
AUX = 32
PAIRS = 8192
STEP = 16
RANGE = 512
N_AUX = 2


def shared_order(key):
    return jax.random.permutation(key, NBLK).astype(jnp.int32)


def draw_block_slot(key, part):
    order = shared_order(key)
    return jnp.argsort(order).astype(jnp.int32)


def draw_pair_table(key, part):
    order = shared_order(key)
    key = jax.random.fold_in(key, 22)
    first_key, second_key, third_key = jax.random.split(key, 3)
    owners = NBLK // BLK_DEV
    device = jnp.arange(PAIRS, dtype=jnp.int32) // PAIR_DEV
    within = jnp.arange(PAIRS, dtype=jnp.int32) % PAIR_DEV
    offset_right = within % (2 * REACH + 1) - REACH
    offset_left = jax.random.randint(first_key, (PAIRS,), -REACH, REACH + 1)
    local_left = jax.random.randint(second_key, (PAIRS,), 0, BLK_DEV)
    local_right = jax.random.randint(third_key, (PAIRS,), 0, BLK_DEV)
    owner_left = jnp.clip(device + offset_left, 0, owners - 1)
    owner_right = jnp.clip(device + offset_right, 0, owners - 1)
    slot_left = owner_left * BLK_DEV + local_left
    slot_right = owner_right * BLK_DEV + local_right
    return jnp.stack([order[slot_left], order[slot_right]], axis=1).astype(jnp.int32)


def domain_offsets(row_key):
    inner_key, place_key = jax.random.split(row_key)
    inner = jax.random.permutation(inner_key, RANGE - 2)[:OCC_DOM - 2].astype(jnp.int32) + 1
    ends = jnp.array([0, RANGE - 1], dtype=jnp.int32)
    joined = jnp.concatenate([inner, ends])
    return jax.random.permutation(place_key, joined).astype(jnp.int32)


def draw_domains(key, part):
    order = shared_order(key)
    key = jax.random.fold_in(key, 23)
    slot_of = jnp.argsort(order).astype(jnp.int32)
    row_keys = jax.random.split(key, NBLK)
    offsets = jax.vmap(domain_offsets)(row_keys)
    return (slot_of[:, None] * STEP + offsets).astype(jnp.int32)


def block_levels(rng, shape, cuts, smallest, high):
    loudness, own = 1.0, jax.random.fold_in(rng, 6)
    for dim, parts in cuts:
        steps = jnp.exp(jax.random.uniform(jax.random.fold_in(own, dim), (parts,), jnp.float32, smallest / len(cuts), high / len(cuts)))
        loudness = loudness * jnp.repeat(steps, shape[dim] // parts).reshape([-1 if axis == dim else 1 for axis in range(len(shape))])
    return loudness


def normal_values(stream_key, extent, deviation, reach, cuts=(), held_as=jnp.bfloat16):
    values = deviation * jax.random.normal(stream_key, extent, jnp.float32)
    if cuts:
        values = values * block_levels(stream_key, extent, cuts, -0.22, 0.18)
    return jnp.clip(values, -reach, reach).astype(held_as)


def setup_inputs(seed: int = 0) -> dict:
    key_list = jax.random.split(jax.random.key(seed), 6)
    return {
        "half_transformed": normal_values(key_list[0], (NBLK, BS, AUX, OCC_DOM), 0.25, 1.5, ((0, 128), (2, 2))),
        "trials": normal_values(key_list[1], (NBLK, BS, NV), 0.008, 0.047851562, ((0, 128),)),
        "pair_table": draw_pair_table(jax.random.fold_in(key_list[5], 71), 0),
        "block_slot": draw_block_slot(jax.random.fold_in(key_list[5], 71), 0),
        "domains": draw_domains(jax.random.fold_in(key_list[5], 71), 0),
    }


def reference(half_transformed, trials, pair_table, block_slot, domains):
    left_slot = block_slot[pair_table[:, 0]].astype(jnp.int32)
    right_slot = block_slot[pair_table[:, 1]].astype(jnp.int32)
    repeated = (pair_table[:, 0] == pair_table[:, 1])
    group_count = PAIRS // 8
    slots_left = left_slot.reshape(group_count, 8)
    slots_right = right_slot.reshape(group_count, 8)
    domains_left = domains[pair_table[:, 0]].reshape(group_count, 8, OCC_DOM)
    domains_right = domains[pair_table[:, 1]].reshape(group_count, 8, OCC_DOM)
    repeat_rows = repeated.reshape(group_count, 8)

    def one_group(result, pair_rows):
        sl, sr, dl, dr, rep = pair_rows
        left_block = half_transformed[sl].astype(jnp.float32)
        right_block = half_transformed[sr].astype(jnp.float32)
        matches = dl[:, :, None] == dr[:, None, :]
        position = jnp.argmax(matches, axis=2).astype(jnp.int32)
        present = jnp.any(matches, axis=2).astype(jnp.float32)
        matched = jnp.take_along_axis(right_block, position[:, None, None, :], axis=3)
        matched = matched * present[:, None, None, :]
        left_vec = trials[sl].astype(jnp.float32)
        right_vec = trials[sr].astype(jnp.float32)
        to_left = jnp.zeros((8, BS, NV), jnp.float32)
        to_right = jnp.zeros((8, BS, NV), jnp.float32)
        for sub_batch in range(N_AUX):
            lower = sub_batch * AUX_DEV
            exchange = jnp.einsum('giPk,gjPk->gij', left_block[:, :, lower:lower + AUX_DEV, :],
                                  matched[:, :, lower:lower + AUX_DEV, :]).astype(jnp.bfloat16)
            exchange = lax.optimization_barrier(exchange).astype(jnp.float32)
            to_left = to_left + jnp.einsum('gij,gjn->gin', exchange, right_vec)
            to_right = to_right + jnp.einsum('gij,gin->gjn', exchange, left_vec)
        keep = 1.0 - rep.astype(jnp.float32)
        result = result.at[sl].add(to_left)
        result = result.at[sr].add(to_right * keep[:, None, None])
        return result, None

    start_value = jnp.zeros((NBLK, BS, NV), jnp.float32)
    applied, unused = lax.scan(one_group, start_value,
                               (slots_left, slots_right, domains_left, domains_right, repeat_rows))
    return applied
```

```python
import jax
import jax.numpy as jnp
from jax import lax
from jax.experimental import pallas as pl
from jax.experimental.pallas import tpu as pltpu
from jax.sharding import PartitionSpec as P

MESH = pl.DeviceIdType.MESH
BS = 128
BLK = 2
PLANE = 16
PLANES = 8
AUXW = 16
HALO = 4
SPAN = 2 * HALO + 1
WIN = PLANE + 2 * HALO
SLOTS = WIN * BLK
MSG = BLK * BS
DEPTH = SPAN * MSG


def dot(a, b, dims=((1,), (0,))):
    return lax.dot_general(a, b, (dims, ((), ())), preferred_element_type=jnp.float32)


def kernel(b_hbm, v_hbm, pt_ref, slot_ref, dom_ref, out_ref,
           braw, vloc, bf32, bt, ysend, yw, cntsend, cnt, nown, nz, nx, domax, dombx, mall,
           wsend, wr, acc, other,
           load_sem, own_sem, cs_sem, cr_sem, ns_sem, nr_sem, ys_sem, yr_sem, zs_sem, zr_sem,
           ws_sem, wr_sem, os_sem, or_sem):
    me = lax.axis_index("pair")
    core = lax.axis_index("aux")
    z = me // PLANE
    g = me % PLANE
    base = z * PLANE
    up = ((z + 1) % PLANES) * PLANE + g
    down = ((z + PLANES - 1) % PLANES) * PLANE + g
    slot_base = base * BLK - HALO * BLK

    def peer(d):
        return (g + d) % PLANE

    load_v = pltpu.make_async_copy(v_hbm, vloc, load_sem.at[0])
    load_b = pltpu.make_async_copy(b_hbm, braw, load_sem.at[1])
    load_v.start()
    load_b.start()

    barrier = pltpu.get_barrier_semaphore()

    def greet(d, carry):
        pl.semaphore_signal(barrier, inc=1, device_id=(base + peer(d), core), device_id_type=MESH)
        return carry

    lax.fori_loop(1, PLANE, greet, 0)
    pl.semaphore_signal(barrier, inc=1, device_id=(up, core), device_id_type=MESH)
    pl.semaphore_signal(barrier, inc=1, device_id=(down, core), device_id_type=MESH)
    pl.semaphore_signal(barrier, inc=1, device_id=(me, 1 - core), device_id_type=MESH)

    slot_row = slot_ref[...]
    pair_rows = pt_ref.shape[0]
    numbers = lax.broadcasted_iota(jnp.int32, (pair_rows, slot_row.shape[1]), 1)
    slot_f = slot_row.astype(jnp.float32)
    pt = pt_ref[...]

    def slot_of(column):
        return jnp.sum(jnp.where(pt[:, column:column + 1] == numbers, slot_f, 0.0), axis=1, keepdims=True)

    slot_a, slot_b = slot_of(0), slot_of(1)
    lane = lax.broadcasted_iota(jnp.int32, (pair_rows, 128), 1).astype(jnp.float32) + slot_base.astype(jnp.float32)
    one_a = (slot_a == lane).astype(jnp.float32)
    one_b = (slot_b == lane).astype(jnp.float32)
    keep = (slot_a != slot_b).astype(jnp.float32)
    counts = dot(one_a.astype(jnp.bfloat16), one_b.astype(jnp.bfloat16), ((0,), (0,)))
    counts = counts + dot((one_b * keep).astype(jnp.bfloat16), one_a.astype(jnp.bfloat16), ((0,), (0,)))
    counts = counts[:SLOTS].astype(jnp.bfloat16)
    cntsend[...] = counts
    cnt[g] = counts

    slot_iota = lax.broadcasted_iota(jnp.int32, (SLOTS, slot_row.shape[1]), 0) + slot_base
    pick = (slot_iota == slot_row).astype(jnp.float32).astype(jnp.bfloat16)
    dom = dom_ref[...]
    dom_high = (dom // 128).astype(jnp.float32).astype(jnp.bfloat16)
    dom_low = (dom % 128).astype(jnp.float32).astype(jnp.bfloat16)
    dom_win = dot(pick, dom_high) * 128.0 + dot(pick, dom_low)
    dom_t = jnp.concatenate([dom_win, jnp.zeros((128 - SLOTS, 128), jnp.float32)], axis=0).T
    for a in range(PLANE * BLK):
        column = dom_t[:, HALO * BLK + a:HALO * BLK + a + 1]
        domax[a] = jnp.broadcast_to(column, (128, 128)).astype(jnp.int32).astype(jnp.int16)
    for s in range(SLOTS):
        dombx[s] = jnp.broadcast_to(dom_win[s:s + 1], (16, 128)).astype(jnp.int32).astype(jnp.int16)

    load_v.wait()
    load_b.wait()
    for k in range(BLK):
        bf32[...] = braw[k].astype(jnp.float32)
        for p in range(AUXW):
            part = bf32[pl.ds(p, BS, stride=AUXW), :].astype(jnp.bfloat16)
            bt[k, p] = part
            ysend[p, k * BS:(k + 1) * BS, :] = dot(part, vloc[k], ((0,), (0,))).astype(jnp.bfloat16)
    own_y = pltpu.make_async_copy(ysend.at[g], yw.at[pl.ds((HALO + g) * MSG, MSG)], own_sem.at[0])
    own_y.start()

    pl.semaphore_wait(barrier, PLANE + 2)

    def count_copy(d, to):
        return pltpu.make_async_remote_copy(
            cntsend, cnt.at[g if to else peer(d)], cs_sem.at[peer(d)], cr_sem.at[g if to else peer(d)],
            device_id=(base + peer(d), core), device_id_type=MESH)

    def y_copy(d, to):
        row = g if to else peer(d)
        return pltpu.make_async_remote_copy(
            ysend.at[peer(d)], yw.at[pl.ds((HALO + row) * MSG, MSG)], ys_sem.at[peer(d)], yr_sem.at[row],
            device_id=(base + peer(d), core), device_id_type=MESH)

    def loop(lower, upper, body):
        def step(d, carry):
            body(d)
            return carry
        lax.fori_loop(lower, upper, step, 0)

    loop(1, PLANE, lambda d: count_copy(d, True).start())
    loop(1, PLANE, lambda d: y_copy(d, True).start())

    loop(1, PLANE, lambda d: count_copy(d, False).wait_recv())
    total = jnp.sum(cnt[...].astype(jnp.float32), axis=0)
    nown[...] = total
    n_up = pltpu.make_async_remote_copy(nown, nz.at[0], ns_sem.at[0], nr_sem.at[0],
                                        device_id=(up, core), device_id_type=MESH)
    n_down = pltpu.make_async_remote_copy(nown, nz.at[1], ns_sem.at[1], nr_sem.at[1],
                                          device_id=(down, core), device_id_type=MESH)
    n_up.start()
    n_down.start()

    def spread(matrix):
        for s in range(SLOTS):
            nx[s] = jnp.broadcast_to(matrix[HALO * BLK:HALO * BLK + PLANE * BLK, s:s + 1], (PLANE * BLK, 128))

    def build(i):
        for k in range(BLK):
            a = i * BLK + k
            left = domax[a]
            for s in range(SPAN * BLK):
                weight = jnp.broadcast_to(nx[i * BLK + s, pl.ds(a, 1), :], (16, 128)).astype(jnp.bfloat16)
                right = dombx[i * BLK + s]
                for h in range(BS // 16):
                    tile = jnp.where(left[h * 16:(h + 1) * 16] == right, weight, jnp.bfloat16(0))
                    mall[i, k * BS + h * 16:k * BS + (h + 1) * 16, s * BS:(s + 1) * BS] = tile

    spread(total)
    loop(HALO, PLANE - HALO, build)

    n_up.wait()
    n_down.wait()
    shift = PLANE * BLK
    wide = SLOTS - shift
    low, high = nz[0], nz[1]
    lanes = lax.broadcasted_iota(jnp.int32, (wide, 128), 1)
    from_low = jnp.where(lanes < wide, pltpu.roll(low[shift:], 128 - shift, 1), 0.0)
    from_high = jnp.where((lanes >= shift) & (lanes < SLOTS), pltpu.roll(high[:wide], shift, 1), 0.0)
    total = total + jnp.concatenate([from_low, jnp.zeros((SLOTS - 2 * wide, 128), jnp.float32), from_high], axis=0)
    spread(total)
    loop(0, HALO, build)
    loop(PLANE - HALO, PLANE, build)

    own_y.wait()

    def wait_y(s):
        @pl.when(s != g)
        def _():
            d = (s + PLANE - g) % PLANE
            y_copy(d, False).wait_recv()

    loop(PLANE - HALO, PLANE, wait_y)
    z_up = pltpu.make_async_remote_copy(
        yw.at[pl.ds(PLANE * MSG, HALO * MSG)], yw.at[pl.ds(0, HALO * MSG)], zs_sem.at[0], zr_sem.at[0],
        device_id=(up, core), device_id_type=MESH)
    z_up.start()
    loop(0, HALO, wait_y)
    z_down = pltpu.make_async_remote_copy(
        yw.at[pl.ds(HALO * MSG, HALO * MSG)], yw.at[pl.ds((HALO + PLANE) * MSG, HALO * MSG)],
        zs_sem.at[1], zr_sem.at[1], device_id=(down, core), device_id_type=MESH)
    z_down.start()
    loop(HALO, PLANE - HALO, wait_y)

    def w_copy(i, source):
        return pltpu.make_async_remote_copy(
            wsend.at[i], wr.at[source], ws_sem.at[i], wr_sem.at[source],
            device_id=(base + i, core), device_id_type=MESH)

    def apply_index(i):
        w = dot(mall[i], yw[pl.ds(i * MSG, DEPTH), :]).astype(jnp.bfloat16)
        wsend[i] = w

        @pl.when(i != g)
        def _():
            w_copy(i, g).start()

    half = PLANE // 2
    loop(0, half, lambda t: apply_index(HALO + (g + t) % half))
    z_up.wait()
    z_down.wait()

    def outer(t):
        j = (g + t) % half
        apply_index(j + half * (j // HALO))

    loop(0, half, outer)

    def add(source):
        def block(k, first):
            return dot(bt[k, source], first)
        for k in range(BLK):
            acc[k] += dot(bt[k, source], wr[source, k * BS:(k + 1) * BS, :])

    own_w = pltpu.make_async_copy(wsend.at[g], wr.at[g], own_sem.at[1])
    own_w.start()
    acc[...] = jnp.zeros_like(acc)
    own_w.wait()
    add(g)

    def collect(t):
        d = PLANE - t
        source = peer(d)
        w_copy(source, source).wait_recv()
        add(source)

    loop(1, PLANE, collect)

    swap = pltpu.make_async_remote_copy(acc, other, os_sem, or_sem,
                                        device_id=(me, 1 - core), device_id_type=MESH)
    swap.start()

    loop(1, PLANE, lambda d: count_copy(d, True).wait_send())
    loop(1, PLANE, lambda d: y_copy(d, True).wait_send())
    loop(1, PLANE, lambda d: w_copy(peer(d), g).wait_send())
    swap.wait()
    out_ref[...] = acc[...] + other[...]


def local(half_transformed, trials, pair_table, block_slot, domains):
    blocks = half_transformed.shape[0]
    vmem = pl.BlockSpec(memory_space=pltpu.VMEM)
    hbm = pl.BlockSpec(memory_space=pl.ANY)
    bf, f32 = jnp.bfloat16, jnp.float32
    dma = pltpu.SemaphoreType.DMA
    scratch = [
        pltpu.VMEM((BLK, BS * AUXW, 128), bf),
        pltpu.VMEM((BLK, BS, 128), bf),
        pltpu.VMEM((BS * AUXW, 128), f32),
        pltpu.VMEM((BLK, AUXW, BS, 128), bf),
        pltpu.VMEM((AUXW, MSG, 128), bf),
        pltpu.VMEM((WIN * MSG, 128), bf),
        pltpu.VMEM((SLOTS, 128), bf),
        pltpu.VMEM((PLANE, SLOTS, 128), bf),
        pltpu.VMEM((SLOTS, 128), f32),
        pltpu.VMEM((2, SLOTS, 128), f32),
        pltpu.VMEM((SLOTS, PLANE * BLK, 128), f32),
        pltpu.VMEM((PLANE * BLK, 128, 128), jnp.int16),
        pltpu.VMEM((SLOTS, 16, 128), jnp.int16),
        pltpu.VMEM((PLANE, MSG, DEPTH), bf),
        pltpu.VMEM((PLANE, MSG, 128), bf),
        pltpu.VMEM((AUXW, MSG, 128), bf),
        pltpu.VMEM((BLK, BS, 128), f32),
        pltpu.VMEM((BLK, BS, 128), f32),
        dma((2,)), dma((2,)), dma((PLANE,)), dma((PLANE,)), dma((2,)), dma((2,)),
        dma((PLANE,)), dma((PLANE,)), dma((2,)), dma((2,)), dma((PLANE,)), dma((PLANE,)), dma, dma,
    ]
    return pl.pallas_call(
        kernel,
        out_shape=jax.ShapeDtypeStruct(trials.shape, f32),
        in_specs=[hbm, hbm, vmem, vmem, vmem],
        out_specs=vmem,
        scratch_shapes=scratch,
        compiler_params=pltpu.CompilerParams(collective_id=1, has_side_effects=True, vmem_limit_bytes=50 << 20),
        name="exchange",
    )(half_transformed.reshape(blocks, BS * AUXW, 128), trials, pair_table,
      block_slot.reshape(1, -1), domains)


def solution(mesh):
    return jax.shard_map(
        local,
        mesh=mesh,
        in_specs=(P("pair", None, "aux", None), P("pair", None, None), P("pair", None), P(), P()),
        out_specs=P("pair", None, None),
        check_vma=False,
    )
```

```python
import jax
import jax.numpy as jnp
from jax import lax
from jax.experimental import pallas as pl
from jax.experimental.pallas import tpu as pltpu
from jax.sharding import PartitionSpec as P

MESH = pl.DeviceIdType.MESH
BS = 128
BLK = 2
PLANE = 16
PLANES = 8
AUXW = 16
HALO = 4
SPAN = 2 * HALO + 1
WIN = PLANE + 2 * HALO
SLOTS = WIN * BLK
EDGE = 2 * HALO * BLK
SIDE = 4
MSG = BLK * BS
DEPTH = SPAN * MSG
ORDER = ((2, 2), (1, 2), (2, 1), (2, 3), (3, 2), (0, 2), (1, 1), (1, 3),
         (2, 0), (3, 1), (3, 3), (0, 1), (0, 3), (1, 0), (3, 0))
TURNS = (2, 1, 3, 0)


def dot(a, b, dims=((1,), (0,))):
    return lax.dot_general(a, b, (dims, ((), ())), preferred_element_type=jnp.float32)


def kernel(b_hbm, v_hbm, pt_hbm, slot_hbm, dom_hbm, out_ref,
           braw, vloc, ptv, slotv, domv, bf32, bt, ysend, yw, cntsend, cnt, nown, nz, nx, domax, dombx, mall,
           wsend, wr, acc, other,
           load_sem, own_sem, cs_sem, cr_sem, ns_sem, nr_sem, ys_sem, yr_sem, zs_sem, zr_sem,
           ws_sem, wr_sem, os_sem, or_sem):
    me = lax.axis_index("pair")
    core = lax.axis_index("aux")
    z = me // PLANE
    g = me % PLANE
    x = g // SIDE
    y = g % SIDE
    base = z * PLANE
    up = ((z + 1) % PLANES) * PLANE + g
    down = ((z + PLANES - 1) % PLANES) * PLANE + g
    slot_base = base * BLK - HALO * BLK

    def moved(d):
        return ((x + d[0]) % SIDE) * SIDE + (y + d[1]) % SIDE

    def source(d):
        return ((x + SIDE - d[0]) % SIDE) * SIDE + (y + SIDE - d[1]) % SIDE

    loads = [pltpu.make_async_copy(a, b, load_sem.at[i]) for i, (a, b) in enumerate(
        ((v_hbm, vloc), (b_hbm, braw), (pt_hbm, ptv), (slot_hbm, slotv), (dom_hbm, domv)))]
    for copy in loads:
        copy.start()

    barrier = pltpu.get_barrier_semaphore()
    for d in ORDER:
        pl.semaphore_signal(barrier, inc=1, device_id=(base + moved(d), core), device_id_type=MESH)
    pl.semaphore_signal(barrier, inc=1, device_id=(up, core), device_id_type=MESH)
    pl.semaphore_signal(barrier, inc=1, device_id=(down, core), device_id_type=MESH)
    pl.semaphore_signal(barrier, inc=1, device_id=(me, 1 - core), device_id_type=MESH)

    for copy in loads:
        copy.wait()

    slot_row = slotv[...]
    blocks = slot_row.shape[1]
    pt = ptv[...]
    numbers = lax.broadcasted_iota(jnp.int32, (blocks, pt.shape[1]), 0)
    named_a = (numbers == pt[0:1]).astype(jnp.float32).astype(jnp.bfloat16)
    named_b = (numbers == pt[1:2]).astype(jnp.float32).astype(jnp.bfloat16)
    keep = (pt[0:1] != pt[1:2]).astype(jnp.float32)

    def pick(rows, first):
        wanted = lax.broadcasted_iota(jnp.int32, (rows, blocks), 0) + first
        return (wanted == slot_row).astype(jnp.float32).astype(jnp.bfloat16)

    pick_plane = pick(128, slot_base)
    pick_own = pick(16, (me - HALO // 2) * BLK)
    rows_a = dot(pick_own, named_a).astype(jnp.bfloat16)
    rows_b = (dot(pick_own, named_b) * keep).astype(jnp.bfloat16)
    cols_a = dot(pick_plane, named_a).astype(jnp.bfloat16)
    cols_b = dot(pick_plane, named_b).astype(jnp.bfloat16)
    counts = dot(rows_a, cols_b, ((1,), (1,))) + dot(rows_b, cols_a, ((1,), (1,)))
    cntsend[...] = counts.astype(jnp.bfloat16)
    cnt[g] = counts.astype(jnp.bfloat16)

    for k in range(BLK):
        bf32[...] = braw[k].astype(jnp.float32)
        for p in range(AUXW):
            part = bf32[pl.ds(p, BS, stride=AUXW), :].astype(jnp.bfloat16)
            bt[k, p] = part
            ysend[p, k * BS:(k + 1) * BS, :] = dot(part, vloc[k], ((0,), (0,))).astype(jnp.bfloat16)
    own_y = pltpu.make_async_copy(ysend.at[g], yw.at[pl.ds((HALO + g) * MSG, MSG)], own_sem.at[0])
    own_y.start()

    pl.semaphore_wait(barrier, PLANE + 2)

    def count_copy(to, row):
        return pltpu.make_async_remote_copy(
            cntsend, cnt.at[row], cs_sem.at[to], cr_sem.at[row],
            device_id=(base + to, core), device_id_type=MESH)

    def y_copy(to, row):
        return pltpu.make_async_remote_copy(
            ysend.at[to], yw.at[pl.ds((HALO + row) * MSG, MSG)], ys_sem.at[to], yr_sem.at[row],
            device_id=(base + to, core), device_id_type=MESH)

    def loop(lower, upper, body):
        def step(d, carry):
            body(d)
            return carry
        lax.fori_loop(lower, upper, step, 0)

    for d in ORDER:
        count_copy(moved(d), g).start()
    for d in ORDER:
        y_copy(moved(d), g).start()

    dom = domv[...]
    dom_high = (dom // 128).astype(jnp.float32).astype(jnp.bfloat16)
    dom_low = (dom % 128).astype(jnp.float32).astype(jnp.bfloat16)
    dom_win = dot(pick_plane, dom_high) * 128.0 + dot(pick_plane, dom_low)
    dom_t = dom_win.T
    for a in range(PLANE * BLK):
        column = dom_t[:, HALO * BLK + a:HALO * BLK + a + 1]
        domax[a] = jnp.broadcast_to(column, (128, 128)).astype(jnp.int32).astype(jnp.int16)
    for s in range(SLOTS):
        dombx[s] = jnp.broadcast_to(dom_win[s:s + 1], (16, 128)).astype(jnp.int32).astype(jnp.int16)

    for d in ORDER:
        count_copy(moved(d), source(d)).wait_recv()
    place_row = lax.broadcasted_iota(jnp.int32, (SLOTS, PLANE * 16), 0)
    place_col = lax.broadcasted_iota(jnp.int32, (SLOTS, PLANE * 16), 1)
    place = (place_row == BLK * (place_col // 16 + HALO // 2) + place_col % 16)
    total = dot(place.astype(jnp.float32).astype(jnp.bfloat16), cnt[...].reshape(PLANE * 16, 128))
    nown[...] = total
    n_up = pltpu.make_async_remote_copy(nown.at[pl.ds(SLOTS - EDGE, EDGE)], nz.at[0], ns_sem.at[0], nr_sem.at[0],
                                        device_id=(up, core), device_id_type=MESH)
    n_down = pltpu.make_async_remote_copy(nown.at[pl.ds(0, EDGE)], nz.at[1], ns_sem.at[1], nr_sem.at[1],
                                          device_id=(down, core), device_id_type=MESH)
    n_up.start()
    n_down.start()

    def spread(matrix):
        for s in range(SLOTS):
            nx[s] = jnp.broadcast_to(matrix[HALO * BLK:HALO * BLK + PLANE * BLK, s:s + 1], (PLANE * BLK, 128))

    def build(i):
        for k in range(BLK):
            a = i * BLK + k
            left = domax[a]
            for s in range(SPAN * BLK):
                weight = jnp.broadcast_to(nx[i * BLK + s, pl.ds(a, 1), :], (16, 128)).astype(jnp.bfloat16)
                right = dombx[i * BLK + s]
                for h in range(BS // 16):
                    tile = jnp.where(left[h * 16:(h + 1) * 16] == right, weight, jnp.bfloat16(0))
                    mall[i, k * BS + h * 16:k * BS + (h + 1) * 16, s * BS:(s + 1) * BS] = tile

    spread(total)
    loop(HALO, PLANE - HALO, build)

    n_up.wait()
    n_down.wait()
    shift = PLANE * BLK
    lanes = lax.broadcasted_iota(jnp.int32, (EDGE, 128), 1)
    from_low = jnp.where(lanes < EDGE, pltpu.roll(nz[0], 128 - shift, 1), 0.0)
    from_high = jnp.where((lanes >= shift) & (lanes < SLOTS), pltpu.roll(nz[1], shift, 1), 0.0)
    total = total + jnp.concatenate([from_low, jnp.zeros((SLOTS - 2 * EDGE, 128), jnp.float32), from_high], axis=0)
    spread(total)
    loop(0, HALO, build)
    loop(PLANE - HALO, PLANE, build)

    def z_copy(upward, n):
        row = (PLANE if upward else HALO) + n
        to = n if upward else HALO + PLANE + n
        side = 0 if upward else 1
        return pltpu.make_async_remote_copy(
            yw.at[pl.ds(row * MSG, MSG)], yw.at[pl.ds(to * MSG, MSG)],
            zs_sem.at[side, n], zr_sem.at[side, n],
            device_id=(up if upward else down, core), device_id_type=MESH)

    def relay(row):
        @pl.when(row >= PLANE - HALO)
        def _():
            z_copy(True, row - (PLANE - HALO)).start()

        @pl.when(row < HALO)
        def _():
            z_copy(False, row).start()

    own_y.wait()
    relay(g)
    for d in ORDER:
        y_copy(moved(d), source(d)).wait_recv()
        relay(source(d))

    def w_copy(i, row):
        return pltpu.make_async_remote_copy(
            wsend.at[i], wr.at[row], ws_sem.at[i], wr_sem.at[row],
            device_id=(base + i, core), device_id_type=MESH)

    def apply_index(i):
        w = dot(mall[i], yw[pl.ds(i * MSG, DEPTH), :]).astype(jnp.bfloat16)
        wsend[i] = w

        @pl.when(i != g)
        def _():
            w_copy(i, g).start()

    side = x // 2

    def turn(t):
        return sum(jnp.where(t == n, TURNS[n], 0) for n in range(SIDE))

    def inner(t):
        row = 2 - side + (t // SIDE) * (2 * side - 1)
        apply_index(row * SIDE + (y + turn(t % SIDE)) % SIDE)

    def outer(t):
        row = 3 - 3 * side + (t // SIDE) * (6 * side - 3)
        apply_index(row * SIDE + (y + turn(t % SIDE)) % SIDE)

    loop(0, 2 * SIDE, inner)
    for n in range(HALO):
        z_copy(True, n).wait()
        z_copy(False, n).wait()
    loop(0, 2 * SIDE, outer)

    def add(row):
        for k in range(BLK):
            acc[k] += dot(bt[k, row], wr[row, k * BS:(k + 1) * BS, :])

    own_w = pltpu.make_async_copy(wsend.at[g], wr.at[g], own_sem.at[1])
    own_w.start()
    acc[...] = jnp.zeros_like(acc)
    own_w.wait()
    add(g)

    def collect(t):
        sender = (2 * (1 - side) + 2 * (t // 8) + t % 2) % SIDE
        row = sender * SIDE + (y + SIDE - turn((t % 8) // 2)) % SIDE

        @pl.when(row != g)
        def _():
            w_copy(row, row).wait_recv()
            add(row)

    loop(0, PLANE, collect)

    swap = pltpu.make_async_remote_copy(acc, other, os_sem, or_sem,
                                        device_id=(me, 1 - core), device_id_type=MESH)
    swap.start()

    for d in ORDER:
        count_copy(moved(d), g).wait_send()
        y_copy(moved(d), g).wait_send()
        w_copy(moved(d), g).wait_send()
    swap.wait()
    out_ref[...] = acc[...] + other[...]


def local(half_transformed, trials, pair_table, block_slot, domains):
    blocks = half_transformed.shape[0]
    count = block_slot.shape[0]
    vmem = pl.BlockSpec(memory_space=pltpu.VMEM)
    hbm = pl.BlockSpec(memory_space=pl.ANY)
    bf, f32 = jnp.bfloat16, jnp.float32
    dma = pltpu.SemaphoreType.DMA
    scratch = [
        pltpu.VMEM((BLK, BS * AUXW, 128), bf),
        pltpu.VMEM((BLK, BS, 128), bf),
        pltpu.VMEM((2, pair_table.shape[0]), jnp.int32),
        pltpu.VMEM((1, count), jnp.int32),
        pltpu.VMEM((count, 128), jnp.int32),
        pltpu.VMEM((BS * AUXW, 128), f32),
        pltpu.VMEM((BLK, AUXW, BS, 128), bf),
        pltpu.VMEM((AUXW, MSG, 128), bf),
        pltpu.VMEM((WIN * MSG, 128), bf),
        pltpu.VMEM((16, 128), bf),
        pltpu.VMEM((PLANE, 16, 128), bf),
        pltpu.VMEM((SLOTS, 128), f32),
        pltpu.VMEM((2, EDGE, 128), f32),
        pltpu.VMEM((SLOTS, PLANE * BLK, 128), f32),
        pltpu.VMEM((PLANE * BLK, 128, 128), jnp.int16),
        pltpu.VMEM((SLOTS, 16, 128), jnp.int16),
        pltpu.VMEM((PLANE, MSG, DEPTH), bf),
        pltpu.VMEM((PLANE, MSG, 128), bf),
        pltpu.VMEM((AUXW, MSG, 128), bf),
        pltpu.VMEM((BLK, BS, 128), f32),
        pltpu.VMEM((BLK, BS, 128), f32),
        dma((5,)), dma((2,)), dma((PLANE,)), dma((PLANE,)), dma((2,)), dma((2,)),
        dma((PLANE,)), dma((PLANE,)), dma((2, HALO)), dma((2, HALO)), dma((PLANE,)), dma((PLANE,)), dma, dma,
    ]
    return pl.pallas_call(
        kernel,
        out_shape=jax.ShapeDtypeStruct(trials.shape, f32),
        in_specs=[hbm] * 5,
        out_specs=vmem,
        scratch_shapes=scratch,
        compiler_params=pltpu.CompilerParams(collective_id=1, has_side_effects=True, vmem_limit_bytes=62 << 20),
        name="exchange",
    )(half_transformed.reshape(blocks, BS * AUXW, 128), trials, pair_table.T,
      block_slot.reshape(1, -1), domains)


def solution(mesh):
    return jax.shard_map(
        local,
        mesh=mesh,
        in_specs=(P("pair", None, "aux", None), P("pair", None, None), P("pair", None), P(), P()),
        out_specs=P("pair", None, None),
        check_vma=False,
    )
```

```python
import jax
import jax.numpy as jnp
from jax import lax
from jax.experimental import pallas as pl
from jax.experimental.pallas import tpu as pltpu
from jax.sharding import PartitionSpec as P

MESH = pl.DeviceIdType.MESH
BS = 128
BLK = 2
PLANE = 16
PLANES = 8
AUXW = 16
HALO = 4
SPAN = 2 * HALO + 1
WIN = PLANE + 2 * HALO
SLOTS = WIN * BLK
EDGE = 2 * HALO * BLK
SIDE = 4
MSG = BLK * BS
OWN = (HALO + 1) * BLK
DEPTH = SPAN * MSG
ORDER = ((2, 2), (1, 2), (2, 1), (2, 3), (3, 2), (0, 2), (1, 1), (1, 3),
         (2, 0), (3, 1), (3, 3), (0, 1), (0, 3), (1, 0), (3, 0))
TURNS = (2, 1, 3, 0)


def dot(a, b, dims=((1,), (0,))):
    return lax.dot_general(a, b, (dims, ((), ())), preferred_element_type=jnp.float32)


def ceil_log2(value):
    return jnp.ceil(jnp.log(value) * 1.4426950408889634)


def halves(value):
    high = value.astype(jnp.bfloat16)
    low = (value - high.astype(jnp.float32)).astype(jnp.bfloat16)
    return jnp.concatenate([high, low], axis=1)


def kernel(b_hbm, v_hbm, pt_hbm, slot_hbm, dom_hbm, out_ref,
           braw, vloc, ptv, slotv, domv, bf32, bt, yf32, ysend, yraw, yw, yunit, wpower, cntsend, cnt, nsend, nz, nx, domax, dombx, mall,
           wsend, wr, wfull, acc, other,
           load_sem, own_sem, cs_sem, cr_sem, ns_sem, nr_sem, ys_sem, yr_sem, zs_sem, zr_sem,
           ws_sem, wr_sem, os_sem, or_sem):
    me = lax.axis_index("pair")
    core = lax.axis_index("aux")
    z = me // PLANE
    g = me % PLANE
    x = g // SIDE
    y = g % SIDE
    base = z * PLANE
    up = ((z + 1) % PLANES) * PLANE + g
    down = ((z + PLANES - 1) % PLANES) * PLANE + g
    slot_base = base * BLK - HALO * BLK

    def moved(d):
        return ((x + d[0]) % SIDE) * SIDE + (y + d[1]) % SIDE

    def source(d):
        return ((x + SIDE - d[0]) % SIDE) * SIDE + (y + SIDE - d[1]) % SIDE

    loads = [pltpu.make_async_copy(a, b, load_sem.at[i]) for i, (a, b) in enumerate(
        ((v_hbm, vloc), (b_hbm, braw), (pt_hbm, ptv), (slot_hbm, slotv), (dom_hbm, domv)))]
    for copy in loads:
        copy.start()

    barrier = pltpu.get_barrier_semaphore()
    for d in ORDER:
        pl.semaphore_signal(barrier, inc=1, device_id=(base + moved(d), core), device_id_type=MESH)
    pl.semaphore_signal(barrier, inc=1, device_id=(up, core), device_id_type=MESH)
    pl.semaphore_signal(barrier, inc=1, device_id=(down, core), device_id_type=MESH)
    pl.semaphore_signal(barrier, inc=1, device_id=(me, 1 - core), device_id_type=MESH)

    for copy in loads:
        copy.wait()

    slot_row = slotv[...]
    blocks = slot_row.shape[1]
    pt = ptv[...]
    numbers = lax.broadcasted_iota(jnp.int32, (blocks, pt.shape[1]), 0)
    named_a = (numbers == pt[0:1]).astype(jnp.float32).astype(jnp.bfloat16)
    named_b = (numbers == pt[1:2]).astype(jnp.float32).astype(jnp.bfloat16)
    keep = (pt[0:1] != pt[1:2]).astype(jnp.float32)

    def pick(rows, first):
        wanted = lax.broadcasted_iota(jnp.int32, (rows, blocks), 0) + first
        return (wanted == slot_row).astype(jnp.float32).astype(jnp.bfloat16)

    pick_plane = pick(128, slot_base)
    pick_own = pick(16, (me - HALO // 2) * BLK)
    rows_a = dot(pick_own, named_a).astype(jnp.bfloat16)
    rows_b = (dot(pick_own, named_b) * keep).astype(jnp.bfloat16)
    cols_a = dot(pick_plane, named_a).astype(jnp.bfloat16)
    cols_b = dot(pick_plane, named_b).astype(jnp.bfloat16)
    counts = dot(rows_a, cols_b, ((1,), (1,))) + dot(rows_b, cols_a, ((1,), (1,)))
    marks = []
    for k in range(BLK):
        bf32[k] = braw[k].astype(jnp.float32)
        top = jnp.full((8, 128), 1e-30, jnp.float32)
        for p in range(AUXW):
            part = bf32[k, pl.ds(p, BS, stride=AUXW), :].astype(jnp.bfloat16)
            bt[k, :, p * BS:(p + 1) * BS] = part
            value = dot(part, vloc[k], ((0,), (0,)))
            yf32[p, k * BS:(k + 1) * BS, :] = value
            top = jnp.maximum(top, jnp.max(jnp.abs(value).reshape(BS // 8, 8, 128), axis=0))
        power = ceil_log2(jnp.max(top, axis=0, keepdims=True) * (1.0 / 32000.0))
        unit = jnp.exp2(-power)
        for p in range(AUXW):
            ysend[p, k * BS:(k + 1) * BS, :] = jnp.round(yf32[p, k * BS:(k + 1) * BS, :] * unit).astype(jnp.int16)
        marks.append(power)
    own_row = lax.broadcasted_iota(jnp.int32, (16, 128), 0)
    counts = jnp.where(own_row == OWN, marks[0], jnp.where(own_row == OWN + 1, marks[1], counts))
    cntsend[...] = counts.astype(jnp.bfloat16)
    cnt[g] = counts.astype(jnp.bfloat16)
    own_y = pltpu.make_async_copy(ysend.at[g], yraw.at[HALO + g], own_sem.at[0])
    own_y.start()

    pl.semaphore_wait(barrier, PLANE + 2)

    def count_copy(to, row):
        return pltpu.make_async_remote_copy(
            cntsend, cnt.at[row], cs_sem.at[to], cr_sem.at[row],
            device_id=(base + to, core), device_id_type=MESH)

    def y_copy(to, row):
        return pltpu.make_async_remote_copy(
            ysend.at[to], yraw.at[HALO + row], ys_sem.at[to], yr_sem.at[row],
            device_id=(base + to, core), device_id_type=MESH)

    def loop(lower, upper, body):
        def step(d, carry):
            body(d)
            return carry
        lax.fori_loop(lower, upper, step, 0)

    for d in ORDER:
        count_copy(moved(d), g).start()
    for d in ORDER:
        y_copy(moved(d), g).start()

    dom = domv[...]
    dom_high = (dom // 128).astype(jnp.float32).astype(jnp.bfloat16)
    dom_low = (dom % 128).astype(jnp.float32).astype(jnp.bfloat16)
    dom_win = dot(pick_plane, dom_high) * 128.0 + dot(pick_plane, dom_low)
    dom_t = dom_win.T
    for a in range(PLANE * BLK):
        column = dom_t[:, HALO * BLK + a:HALO * BLK + a + 1]
        domax[a] = jnp.broadcast_to(column, (128, 128)).astype(jnp.int32).astype(jnp.int16)
    for s in range(SLOTS):
        dombx[s] = jnp.broadcast_to(dom_win[s:s + 1], (16, 128)).astype(jnp.int32).astype(jnp.int16)

    for d in ORDER:
        count_copy(moved(d), source(d)).wait_recv()
    place_row = lax.broadcasted_iota(jnp.int32, (SLOTS, PLANE * 16), 0)
    place_col = lax.broadcasted_iota(jnp.int32, (SLOTS, PLANE * 16), 1)
    place_own = place_col % 16
    place = (place_row == BLK * (place_col // 16 + HALO // 2) + place_own) & (place_own < OWN)
    place_power = (place_row == BLK * (place_col // 16 + HALO) + place_own - OWN) & (place_own >= OWN) & (place_own < OWN + BLK)
    messages = cnt[...].reshape(PLANE * 16, 128)
    total = dot(place.astype(jnp.float32).astype(jnp.bfloat16), messages)
    power = dot(place_power.astype(jnp.float32).astype(jnp.bfloat16), messages)
    nsend[0] = jnp.concatenate([total[SLOTS - EDGE:], power[SLOTS - EDGE:SLOTS - EDGE // 2]], axis=0)
    nsend[1] = jnp.concatenate([total[:EDGE], power[EDGE // 2:EDGE]], axis=0)
    n_up = pltpu.make_async_remote_copy(nsend.at[0], nz.at[0], ns_sem.at[0], nr_sem.at[0],
                                        device_id=(up, core), device_id_type=MESH)
    n_down = pltpu.make_async_remote_copy(nsend.at[1], nz.at[1], ns_sem.at[1], nr_sem.at[1],
                                          device_id=(down, core), device_id_type=MESH)
    n_up.start()
    n_down.start()

    def spread(matrix):
        rows = matrix[HALO * BLK:HALO * BLK + PLANE * BLK]
        half = jnp.where(rows > 256.0, 0.5, 0.0)
        for n, side_of in enumerate((rows - half, rows + half)):
            for s in range(SLOTS):
                nx[n, s] = jnp.broadcast_to(side_of[:, s:s + 1], (PLANE * BLK, 128))

    def build(i):
        for k in range(BLK):
            a = i * BLK + k
            left = domax[a]
            for s in range(SPAN * BLK):
                weight = [jnp.broadcast_to(nx[n, i * BLK + s, pl.ds(a, 1), :], (16, 128)).astype(jnp.bfloat16)
                          for n in range(2)]
                right = dombx[i * BLK + s]
                for h in range(BS // 16):
                    tile = jnp.where(left[h * 16:(h + 1) * 16] == right, weight[h % 2], jnp.bfloat16(0))
                    mall[i, k * BS + h * 16:k * BS + (h + 1) * 16, s * BS:(s + 1) * BS] = tile

    spread(total)
    loop(HALO, PLANE - HALO, build)

    n_up.wait()
    n_down.wait()
    shift = PLANE * BLK
    lanes = lax.broadcasted_iota(jnp.int32, (EDGE, 128), 1)
    from_low = jnp.where(lanes < EDGE, pltpu.roll(nz[0, :EDGE], 128 - shift, 1), 0.0)
    from_high = jnp.where((lanes >= shift) & (lanes < SLOTS), pltpu.roll(nz[1, :EDGE], shift, 1), 0.0)
    total = total + jnp.concatenate([from_low, jnp.zeros((SLOTS - 2 * EDGE, 128), jnp.float32), from_high], axis=0)
    spread(total)
    power = jnp.concatenate([nz[0, EDGE:], power[EDGE // 2:SLOTS - EDGE // 2], nz[1, EDGE:]], axis=0)
    units = jnp.exp2(power)
    yunit[...] = units
    units = jnp.concatenate([units, jnp.zeros((128 - SLOTS, 128), jnp.float32)], axis=0).astype(jnp.bfloat16)
    bound = dot(total[HALO * BLK:HALO * BLK + PLANE * BLK].astype(jnp.bfloat16), units)
    wpower[...] = ceil_log2(jnp.maximum(bound, 1e-35) * 1.001)
    loop(0, HALO, build)
    loop(PLANE - HALO, PLANE, build)

    def z_copy(upward, n):
        row = (PLANE if upward else HALO) + n
        to = n if upward else HALO + PLANE + n
        side = 0 if upward else 1
        return pltpu.make_async_remote_copy(
            yraw.at[row], yraw.at[to],
            zs_sem.at[side, n], zr_sem.at[side, n],
            device_id=(up if upward else down, core), device_id_type=MESH)

    def relay(row):
        @pl.when(row >= PLANE - HALO)
        def _():
            z_copy(True, row - (PLANE - HALO)).start()

        @pl.when(row < HALO)
        def _():
            z_copy(False, row).start()

    def unpack(w):
        for k in range(BLK):
            value = yraw[w, k * BS:(k + 1) * BS, :].astype(jnp.float32) * yunit[pl.ds(w * BLK + k, 1), :]
            yw[pl.ds(w * MSG + k * BS, BS), :] = halves(value)

    def step(t):
        code = sum(jnp.where(t == n, SIDE * d[0] + d[1], 0) for n, d in enumerate(ORDER))
        return code // SIDE, code % SIDE

    own_y.wait()
    relay(g)
    unpack(HALO + g)

    def arrive(t):
        row = source(step(t))
        y_copy(row, row).wait_recv()
        relay(row)
        unpack(HALO + row)

    loop(0, PLANE - 1, arrive)

    def w_copy(i, row):
        return pltpu.make_async_remote_copy(
            wsend.at[i], wr.at[row], ws_sem.at[i], wr_sem.at[row],
            device_id=(base + i, core), device_id_type=MESH)

    def apply_index(i):
        both = dot(mall[i], yw[pl.ds(i * MSG, DEPTH), :])
        for k in range(BLK):
            part = both[k * BS:(k + 1) * BS]
            unit = jnp.exp2(-wpower[pl.ds(i * BLK + k, 1), :])
            wsend[i, k * BS:(k + 1) * BS, :] = jnp.round((part[:, :128] + part[:, 128:]) * unit).astype(jnp.int16)

        @pl.when(i != g)
        def _():
            w_copy(i, g).start()

    side = x // 2

    def turn(t):
        return sum(jnp.where(t == n, TURNS[n], 0) for n in range(SIDE))

    def inner(t):
        row = 2 - side + (t // SIDE) * (2 * side - 1)
        apply_index(row * SIDE + (y + turn(t % SIDE)) % SIDE)

    def outer(t):
        row = 3 - 3 * side + (t // SIDE) * (6 * side - 3)
        apply_index(row * SIDE + (y + turn(t % SIDE)) % SIDE)

    loop(0, 2 * SIDE, inner)
    for n in range(HALO):
        z_copy(True, n).wait()
        z_copy(False, n).wait()
        unpack(n)
        unpack(HALO + PLANE + n)
    loop(0, 2 * SIDE, outer)

    def gather(row):
        for k in range(BLK):
            wfull[k, pl.ds(row * BS, BS), :] = halves(wr[row, k * BS:(k + 1) * BS, :].astype(jnp.float32))

    own_w = pltpu.make_async_copy(wsend.at[g], wr.at[g], own_sem.at[1])
    own_w.start()
    own_w.wait()
    gather(g)

    def collect(t, first):
        sender = first + t % 2
        row = sender * SIDE + (y + SIDE - turn(t // 2)) % SIDE

        @pl.when(row != g)
        def _():
            w_copy(row, row).wait_recv()
            gather(row)

    half = AUXW * BS // 2
    for n in range(2):
        first = 2 * ((side + 1 + n) % 2)
        loop(0, 2 * SIDE, lambda t: collect(t, first))
        depth = pl.ds(pl.multiple_of(first // 2 * half, half), half)
        for k in range(BLK):
            both = dot(bt[k, :, depth], wfull[k, depth, :])
            part = both[:, :128] + both[:, 128:]
            acc[k] = part if n == 0 else acc[k] + part

    for k in range(BLK):
        acc[k] = acc[k] * jnp.exp2(wpower[pl.ds(g * BLK + k, 1), :])
    swap = pltpu.make_async_remote_copy(acc, other, os_sem, or_sem,
                                        device_id=(me, 1 - core), device_id_type=MESH)
    swap.start()

    for d in ORDER:
        count_copy(moved(d), g).wait_send()
        y_copy(moved(d), g).wait_send()
        w_copy(moved(d), g).wait_send()
    swap.wait()
    out_ref[...] = acc[...] + other[...]


def local(half_transformed, trials, pair_table, block_slot, domains):
    blocks = half_transformed.shape[0]
    count = block_slot.shape[0]
    vmem = pl.BlockSpec(memory_space=pltpu.VMEM)
    hbm = pl.BlockSpec(memory_space=pl.ANY)
    bf, f32 = jnp.bfloat16, jnp.float32
    dma = pltpu.SemaphoreType.DMA
    scratch = [
        pltpu.VMEM((BLK, BS * AUXW, 128), bf),
        pltpu.VMEM((BLK, BS, 128), bf),
        pltpu.VMEM((2, pair_table.shape[0]), jnp.int32),
        pltpu.VMEM((1, count), jnp.int32),
        pltpu.VMEM((count, 128), jnp.int32),
        pltpu.VMEM((BLK, BS * AUXW, 128), f32),
        pltpu.VMEM((BLK, BS, AUXW * 128), bf),
        pltpu.VMEM((AUXW, MSG, 128), f32),
        pltpu.VMEM((AUXW, MSG, 128), jnp.int16),
        pltpu.VMEM((WIN, MSG, 128), jnp.int16),
        pltpu.VMEM((WIN * MSG, 256), bf),
        pltpu.VMEM((SLOTS, 128), f32),
        pltpu.VMEM((PLANE * BLK, 128), f32),
        pltpu.VMEM((16, 128), bf),
        pltpu.VMEM((PLANE, 16, 128), bf),
        pltpu.VMEM((2, EDGE + EDGE // 2, 128), f32),
        pltpu.VMEM((2, EDGE + EDGE // 2, 128), f32),
        pltpu.VMEM((2, SLOTS, PLANE * BLK, 128), f32),
        pltpu.VMEM((PLANE * BLK, 128, 128), jnp.int16),
        pltpu.VMEM((SLOTS, 16, 128), jnp.int16),
        pltpu.VMEM((PLANE, MSG, DEPTH), bf),
        pltpu.VMEM((PLANE, MSG, 128), jnp.int16),
        pltpu.VMEM((AUXW, MSG, 128), jnp.int16),
        pltpu.VMEM((BLK, AUXW * 128, 256), bf),
        pltpu.VMEM((BLK, BS, 128), f32),
        pltpu.VMEM((BLK, BS, 128), f32),
        dma((5,)), dma((2,)), dma((PLANE,)), dma((PLANE,)), dma((2,)), dma((2,)),
        dma((PLANE,)), dma((PLANE,)), dma((2, HALO)), dma((2, HALO)), dma((PLANE,)), dma((PLANE,)), dma, dma,
    ]
    return pl.pallas_call(
        kernel,
        out_shape=jax.ShapeDtypeStruct(trials.shape, f32),
        in_specs=[hbm] * 5,
        out_specs=vmem,
        scratch_shapes=scratch,
        compiler_params=pltpu.CompilerParams(collective_id=1, has_side_effects=True, vmem_limit_bytes=62 << 20),
        name="exchange",
    )(half_transformed.reshape(blocks, BS * AUXW, 128), trials, pair_table.T,
      block_slot.reshape(1, -1), domains)


def solution(mesh):
    return jax.shard_map(
        local,
        mesh=mesh,
        in_specs=(P("pair", None, "aux", None), P("pair", None, None), P("pair", None), P(), P()),
        out_specs=P("pair", None, None),
        check_vma=False,
    )
```

```python
import jax
import jax.numpy as jnp
from jax import lax
from jax.experimental import pallas as pl
from jax.experimental.pallas import tpu as pltpu
from jax.sharding import PartitionSpec as P

MESH = pl.DeviceIdType.MESH
BS = 128
BLK = 2
PLANE = 16
PLANES = 8
AUXW = 16
HALO = 4
SPAN = 2 * HALO + 1
WIN = PLANE + 2 * HALO
SLOTS = WIN * BLK
EDGE = 2 * HALO * BLK
SIDE = 4
MSG = BLK * BS
OWN = (HALO + 1) * BLK
DEPTH = SPAN * MSG
ORDER = ((2, 2), (1, 2), (2, 1), (2, 3), (3, 2), (0, 2), (1, 1), (1, 3),
         (2, 0), (3, 1), (3, 3), (0, 1), (0, 3), (1, 0), (3, 0))
TURNS = (2, 1, 3, 0)


def dot(a, b, dims=((1,), (0,))):
    return lax.dot_general(a, b, (dims, ((), ())), preferred_element_type=jnp.float32)


def ceil_log2(value):
    return jnp.ceil(jnp.log(value) * 1.4426950408889634)


def halves(value):
    high = value.astype(jnp.bfloat16)
    low = (value - high.astype(jnp.float32)).astype(jnp.bfloat16)
    return jnp.concatenate([high, low], axis=1)


def kernel(b_hbm, v_hbm, pt_hbm, slot_hbm, dom_hbm, out_ref,
           braw, vloc, ptv, slotv, domv, bf32, bt, yf32, ysend, yraw, yw, yunit, wpower, cntsend, cnt, nsend, nz, nx, domax, dombx, mall,
           wsend, wr, wfull, acc, other,
           load_sem, own_sem, cs_sem, cr_sem, ns_sem, nr_sem, ys_sem, yr_sem, zs_sem, zr_sem,
           ws_sem, wr_sem, os_sem, or_sem):
    me = lax.axis_index("pair")
    core = lax.axis_index("aux")
    z = me // PLANE
    g = me % PLANE
    x = g // SIDE
    y = g % SIDE
    base = z * PLANE
    up = ((z + 1) % PLANES) * PLANE + g
    down = ((z + PLANES - 1) % PLANES) * PLANE + g
    slot_base = base * BLK - HALO * BLK

    def moved(d):
        return ((x + d[0]) % SIDE) * SIDE + (y + d[1]) % SIDE

    def source(d):
        return ((x + SIDE - d[0]) % SIDE) * SIDE + (y + SIDE - d[1]) % SIDE

    loads = [pltpu.make_async_copy(a, b, load_sem.at[i]) for i, (a, b) in enumerate(
        ((pt_hbm, ptv), (slot_hbm, slotv), (v_hbm, vloc), (b_hbm, braw), (dom_hbm, domv)))]
    for copy in loads:
        copy.start()

    barrier = pltpu.get_barrier_semaphore()
    for d in ORDER:
        pl.semaphore_signal(barrier, inc=1, device_id=(base + moved(d), core), device_id_type=MESH)
    pl.semaphore_signal(barrier, inc=1, device_id=(up, core), device_id_type=MESH)
    pl.semaphore_signal(barrier, inc=1, device_id=(down, core), device_id_type=MESH)
    pl.semaphore_signal(barrier, inc=1, device_id=(me, 1 - core), device_id_type=MESH)

    load_pairs, load_slots, load_v, load_b, load_domains = loads
    load_pairs.wait()
    load_slots.wait()

    slot_row = slotv[...]
    blocks = slot_row.shape[1]
    pt = ptv[...]
    numbers = lax.broadcasted_iota(jnp.int32, (blocks, pt.shape[1]), 0)
    named_a = (numbers == pt[0:1]).astype(jnp.float32).astype(jnp.bfloat16)
    named_b = (numbers == pt[1:2]).astype(jnp.float32).astype(jnp.bfloat16)
    keep = (pt[0:1] != pt[1:2]).astype(jnp.float32)

    def pick(rows, first):
        wanted = lax.broadcasted_iota(jnp.int32, (rows, blocks), 0) + first
        return (wanted == slot_row).astype(jnp.float32).astype(jnp.bfloat16)

    pick_plane = pick(128, slot_base)
    pick_own = pick(16, (me - HALO // 2) * BLK)
    rows_a = dot(pick_own, named_a).astype(jnp.bfloat16)
    rows_b = (dot(pick_own, named_b) * keep).astype(jnp.bfloat16)
    cols_a = dot(pick_plane, named_a).astype(jnp.bfloat16)
    cols_b = dot(pick_plane, named_b).astype(jnp.bfloat16)
    counts = dot(rows_a, cols_b, ((1,), (1,))) + dot(rows_b, cols_a, ((1,), (1,)))
    load_v.wait()
    load_b.wait()
    marks = []
    for k in range(BLK):
        bf32[k] = braw[k].astype(jnp.float32)
        top = jnp.full((8, 128), 1e-30, jnp.float32)
        for p in range(AUXW):
            part = bf32[k, pl.ds(p, BS, stride=AUXW), :].astype(jnp.bfloat16)
            bt[k, :, p * BS:(p + 1) * BS] = part
            value = dot(part, vloc[k], ((0,), (0,)))
            yf32[p, k * BS:(k + 1) * BS, :] = value
            top = jnp.maximum(top, jnp.max(jnp.abs(value).reshape(BS // 8, 8, 128), axis=0))
        power = ceil_log2(jnp.max(top, axis=0, keepdims=True) * (1.0 / 32000.0))
        unit = jnp.exp2(-power)
        for p in range(AUXW):
            ysend[p, k * BS:(k + 1) * BS, :] = jnp.round(yf32[p, k * BS:(k + 1) * BS, :] * unit).astype(jnp.int16)
        marks.append(power)
    own_row = lax.broadcasted_iota(jnp.int32, (16, 128), 0)
    counts = jnp.where(own_row == OWN, marks[0], jnp.where(own_row == OWN + 1, marks[1], counts))
    cntsend[...] = counts.astype(jnp.bfloat16)
    cnt[g] = counts.astype(jnp.bfloat16)
    own_y = pltpu.make_async_copy(ysend.at[g], yraw.at[HALO + g], own_sem.at[0])
    own_y.start()

    pl.semaphore_wait(barrier, PLANE + 2)

    def count_copy(to, row):
        return pltpu.make_async_remote_copy(
            cntsend, cnt.at[row], cs_sem.at[to], cr_sem.at[row],
            device_id=(base + to, core), device_id_type=MESH)

    def y_copy(to, row):
        return pltpu.make_async_remote_copy(
            ysend.at[to], yraw.at[HALO + row], ys_sem.at[to], yr_sem.at[row],
            device_id=(base + to, core), device_id_type=MESH)

    def loop(lower, upper, body):
        def step(d, carry):
            body(d)
            return carry
        lax.fori_loop(lower, upper, step, 0)

    for d in ORDER:
        count_copy(moved(d), g).start()
    for d in ORDER:
        y_copy(moved(d), g).start()

    load_domains.wait()
    dom = domv[...]
    dom_high = (dom // 128).astype(jnp.float32).astype(jnp.bfloat16)
    dom_low = (dom % 128).astype(jnp.float32).astype(jnp.bfloat16)
    dom_win = dot(pick_plane, dom_high) * 128.0 + dot(pick_plane, dom_low)
    dom_t = dom_win.T
    for a in range(PLANE * BLK):
        column = dom_t[:, HALO * BLK + a:HALO * BLK + a + 1]
        domax[a] = jnp.broadcast_to(column, (128, 128)).astype(jnp.int32).astype(jnp.int16)
    for s in range(SLOTS):
        dombx[s] = jnp.broadcast_to(dom_win[s:s + 1], (16, 128)).astype(jnp.int32).astype(jnp.int16)

    for d in ORDER:
        count_copy(moved(d), source(d)).wait_recv()
    place_row = lax.broadcasted_iota(jnp.int32, (SLOTS, PLANE * 16), 0)
    place_col = lax.broadcasted_iota(jnp.int32, (SLOTS, PLANE * 16), 1)
    place_own = place_col % 16
    place = (place_row == BLK * (place_col // 16 + HALO // 2) + place_own) & (place_own < OWN)
    place_power = (place_row == BLK * (place_col // 16 + HALO) + place_own - OWN) & (place_own >= OWN) & (place_own < OWN + BLK)
    messages = cnt[...].reshape(PLANE * 16, 128)
    total = dot(place.astype(jnp.float32).astype(jnp.bfloat16), messages)
    power = dot(place_power.astype(jnp.float32).astype(jnp.bfloat16), messages)
    nsend[0] = jnp.concatenate([total[SLOTS - EDGE:], power[SLOTS - EDGE:SLOTS - EDGE // 2]], axis=0)
    nsend[1] = jnp.concatenate([total[:EDGE], power[EDGE // 2:EDGE]], axis=0)
    n_up = pltpu.make_async_remote_copy(nsend.at[0], nz.at[0], ns_sem.at[0], nr_sem.at[0],
                                        device_id=(up, core), device_id_type=MESH)
    n_down = pltpu.make_async_remote_copy(nsend.at[1], nz.at[1], ns_sem.at[1], nr_sem.at[1],
                                          device_id=(down, core), device_id_type=MESH)
    n_up.start()
    n_down.start()

    def spread(matrix):
        rows = matrix[HALO * BLK:HALO * BLK + PLANE * BLK]
        half = jnp.where(rows > 256.0, 0.5, 0.0)
        for n, side_of in enumerate((rows - half, rows + half)):
            for s in range(SLOTS):
                nx[n, s] = jnp.broadcast_to(side_of[:, s:s + 1], (PLANE * BLK, 128))

    def build(i):
        for k in range(BLK):
            a = i * BLK + k
            left = domax[a]
            for s in range(SPAN * BLK):
                weight = [jnp.broadcast_to(nx[n, i * BLK + s, pl.ds(a, 1), :], (16, 128)).astype(jnp.bfloat16)
                          for n in range(2)]
                right = dombx[i * BLK + s]
                for h in range(BS // 16):
                    tile = jnp.where(left[h * 16:(h + 1) * 16] == right, weight[h % 2], jnp.bfloat16(0))
                    mall[i, k * BS + h * 16:k * BS + (h + 1) * 16, s * BS:(s + 1) * BS] = tile

    spread(total)
    loop(HALO, PLANE - HALO, build)

    n_up.wait()
    n_down.wait()
    shift = PLANE * BLK
    lanes = lax.broadcasted_iota(jnp.int32, (EDGE, 128), 1)
    from_low = jnp.where(lanes < EDGE, pltpu.roll(nz[0, :EDGE], 128 - shift, 1), 0.0)
    from_high = jnp.where((lanes >= shift) & (lanes < SLOTS), pltpu.roll(nz[1, :EDGE], shift, 1), 0.0)
    total = total + jnp.concatenate([from_low, jnp.zeros((SLOTS - 2 * EDGE, 128), jnp.float32), from_high], axis=0)
    spread(total)
    power = jnp.concatenate([nz[0, EDGE:], power[EDGE // 2:SLOTS - EDGE // 2], nz[1, EDGE:]], axis=0)
    units = jnp.exp2(power)
    yunit[...] = units
    units = jnp.concatenate([units, jnp.zeros((128 - SLOTS, 128), jnp.float32)], axis=0).astype(jnp.bfloat16)
    bound = dot(total[HALO * BLK:HALO * BLK + PLANE * BLK].astype(jnp.bfloat16), units)
    wpower[...] = ceil_log2(jnp.maximum(bound, 1e-35) * 1.001)

    def z_copy(upward, n):
        row = (PLANE if upward else HALO) + n
        to = n if upward else HALO + PLANE + n
        side = 0 if upward else 1
        return pltpu.make_async_remote_copy(
            yraw.at[row], yraw.at[to],
            zs_sem.at[side, n], zr_sem.at[side, n],
            device_id=(up if upward else down, core), device_id_type=MESH)

    def relay(row):
        @pl.when(row >= PLANE - HALO)
        def _():
            z_copy(True, row - (PLANE - HALO)).start()

        @pl.when(row < HALO)
        def _():
            z_copy(False, row).start()

    def unpack(w):
        for k in range(BLK):
            value = yraw[w, k * BS:(k + 1) * BS, :].astype(jnp.float32) * yunit[pl.ds(w * BLK + k, 1), :]
            yw[pl.ds(w * MSG + k * BS, BS), :] = halves(value)

    def step(t):
        code = sum(jnp.where(t == n, SIDE * d[0] + d[1], 0) for n, d in enumerate(ORDER))
        return code // SIDE, code % SIDE

    own_y.wait()
    relay(g)
    unpack(HALO + g)

    def arrive(t):
        row = source(step(t))
        y_copy(row, row).wait_recv()
        relay(row)
        unpack(HALO + row)

    loop(0, 5, arrive)
    loop(0, HALO, build)
    loop(PLANE - HALO, PLANE, build)
    loop(5, PLANE - 1, arrive)

    def w_copy(i, row):
        return pltpu.make_async_remote_copy(
            wsend.at[i], wr.at[row], ws_sem.at[i], wr_sem.at[row],
            device_id=(base + i, core), device_id_type=MESH)

    def apply_index(i):
        both = dot(mall[i], yw[pl.ds(i * MSG, DEPTH), :])
        for k in range(BLK):
            part = both[k * BS:(k + 1) * BS]
            unit = jnp.exp2(-wpower[pl.ds(i * BLK + k, 1), :])
            wsend[i, k * BS:(k + 1) * BS, :] = jnp.round((part[:, :128] + part[:, 128:]) * unit).astype(jnp.int16)

        @pl.when(i != g)
        def _():
            w_copy(i, g).start()

    side = x // 2

    def turn(t):
        return sum(jnp.where(t == n, TURNS[n], 0) for n in range(SIDE))

    def inner(t):
        row = 2 - side + (t // SIDE) * (2 * side - 1)
        apply_index(row * SIDE + (y + turn(t % SIDE)) % SIDE)

    def outer(t):
        row = 3 - 3 * side + (t // SIDE) * (6 * side - 3)
        apply_index(row * SIDE + (y + turn(t % SIDE)) % SIDE)

    loop(0, 2 * SIDE, inner)
    for n in range(HALO):
        z_copy(True, n).wait()
        z_copy(False, n).wait()
        unpack(n)
        unpack(HALO + PLANE + n)
    loop(0, 2 * SIDE, outer)

    def gather(row):
        for k in range(BLK):
            wfull[k, pl.ds(row * BS, BS), :] = halves(wr[row, k * BS:(k + 1) * BS, :].astype(jnp.float32))

    own_w = pltpu.make_async_copy(wsend.at[g], wr.at[g], own_sem.at[1])
    own_w.start()
    own_w.wait()
    gather(g)

    def collect(t, first):
        sender = first + t % 2
        row = sender * SIDE + (y + SIDE - turn(t // 2)) % SIDE

        @pl.when(row != g)
        def _():
            w_copy(row, row).wait_recv()
            gather(row)

    half = AUXW * BS // 2
    for n in range(2):
        first = 2 * ((side + 1 + n) % 2)
        loop(0, 2 * SIDE, lambda t: collect(t, first))
        depth = pl.ds(pl.multiple_of(first // 2 * half, half), half)
        for k in range(BLK):
            both = dot(bt[k, :, depth], wfull[k, depth, :])
            part = both[:, :128] + both[:, 128:]
            acc[k] = part if n == 0 else acc[k] + part

    for k in range(BLK):
        acc[k] = acc[k] * jnp.exp2(wpower[pl.ds(g * BLK + k, 1), :])
    swap = pltpu.make_async_remote_copy(acc, other, os_sem, or_sem,
                                        device_id=(me, 1 - core), device_id_type=MESH)
    swap.start()

    for d in ORDER:
        count_copy(moved(d), g).wait_send()
        y_copy(moved(d), g).wait_send()
        w_copy(moved(d), g).wait_send()
    swap.wait()
    out_ref[...] = acc[...] + other[...]


def local(half_transformed, trials, pair_table, block_slot, domains):
    blocks = half_transformed.shape[0]
    count = block_slot.shape[0]
    vmem = pl.BlockSpec(memory_space=pltpu.VMEM)
    hbm = pl.BlockSpec(memory_space=pl.ANY)
    bf, f32 = jnp.bfloat16, jnp.float32
    dma = pltpu.SemaphoreType.DMA
    scratch = [
        pltpu.VMEM((BLK, BS * AUXW, 128), bf),
        pltpu.VMEM((BLK, BS, 128), bf),
        pltpu.VMEM((2, pair_table.shape[0]), jnp.int32),
        pltpu.VMEM((1, count), jnp.int32),
        pltpu.VMEM((count, 128), jnp.int32),
        pltpu.VMEM((BLK, BS * AUXW, 128), f32),
        pltpu.VMEM((BLK, BS, AUXW * 128), bf),
        pltpu.VMEM((AUXW, MSG, 128), f32),
        pltpu.VMEM((AUXW, MSG, 128), jnp.int16),
        pltpu.VMEM((WIN, MSG, 128), jnp.int16),
        pltpu.VMEM((WIN * MSG, 256), bf),
        pltpu.VMEM((SLOTS, 128), f32),
        pltpu.VMEM((PLANE * BLK, 128), f32),
        pltpu.VMEM((16, 128), bf),
        pltpu.VMEM((PLANE, 16, 128), bf),
        pltpu.VMEM((2, EDGE + EDGE // 2, 128), f32),
        pltpu.VMEM((2, EDGE + EDGE // 2, 128), f32),
        pltpu.VMEM((2, SLOTS, PLANE * BLK, 128), f32),
        pltpu.VMEM((PLANE * BLK, 128, 128), jnp.int16),
        pltpu.VMEM((SLOTS, 16, 128), jnp.int16),
        pltpu.VMEM((PLANE, MSG, DEPTH), bf),
        pltpu.VMEM((PLANE, MSG, 128), jnp.int16),
        pltpu.VMEM((AUXW, MSG, 128), jnp.int16),
        pltpu.VMEM((BLK, AUXW * 128, 256), bf),
        pltpu.VMEM((BLK, BS, 128), f32),
        pltpu.VMEM((BLK, BS, 128), f32),
        dma((5,)), dma((2,)), dma((PLANE,)), dma((PLANE,)), dma((2,)), dma((2,)),
        dma((PLANE,)), dma((PLANE,)), dma((2, HALO)), dma((2, HALO)), dma((PLANE,)), dma((PLANE,)), dma, dma,
    ]
    return pl.pallas_call(
        kernel,
        out_shape=jax.ShapeDtypeStruct(trials.shape, f32),
        in_specs=[hbm] * 5,
        out_specs=vmem,
        scratch_shapes=scratch,
        compiler_params=pltpu.CompilerParams(collective_id=1, has_side_effects=True, vmem_limit_bytes=62 << 20),
        name="exchange",
    )(half_transformed.reshape(blocks, BS * AUXW, 128), trials, pair_table.T,
      block_slot.reshape(1, -1), domains)


def solution(mesh):
    return jax.shard_map(
        local,
        mesh=mesh,
        in_specs=(P("pair", None, "aux", None), P("pair", None, None), P("pair", None), P(), P()),
        out_specs=P("pair", None, None),
        check_vma=False,
    )
```

```python
import jax
import jax.numpy as jnp
from jax import lax
from jax.experimental import pallas as pl
from jax.experimental.pallas import tpu as pltpu
from jax.sharding import PartitionSpec as P

MESH = pl.DeviceIdType.MESH
BS = 128
BLK = 2
PLANE = 16
PLANES = 8
AUXW = 16
HALO = 4
SPAN = 2 * HALO + 1
WIN = PLANE + 2 * HALO
SLOTS = WIN * BLK
EDGE = 2 * HALO * BLK
SIDE = 4
MSG = BLK * BS
OWN = (HALO + 1) * BLK
DEPTH = SPAN * MSG
ORDER = ((2, 2), (1, 2), (2, 1), (2, 3), (3, 2), (0, 2), (1, 1), (1, 3),
         (2, 0), (3, 1), (3, 3), (0, 1), (0, 3), (1, 0), (3, 0))
TURNS = (2, 1, 3, 0)


def dot(a, b, dims=((1,), (0,))):
    return lax.dot_general(a, b, (dims, ((), ())), preferred_element_type=jnp.float32)


def ceil_log2(value):
    return jnp.ceil(jnp.log(value) * 1.4426950408889634)


def halves(value):
    high = value.astype(jnp.bfloat16)
    low = (value - high.astype(jnp.float32)).astype(jnp.bfloat16)
    return jnp.concatenate([high, low], axis=1)


def kernel(b_hbm, v_hbm, pt_hbm, slot_hbm, dom_hbm, out_ref,
           braw, vloc, ptv, slotv, domv, bf32, bt, yf32, ysend, yraw, yw, yunit, wpower, cntsend, cnt, nsend, nz, nx, domax, dombx, mall,
           wsend, wr, wfull, acc, other,
           load_sem, own_sem, cs_sem, cr_sem, ns_sem, nr_sem, ys_sem, yr_sem, zs_sem, zr_sem,
           ws_sem, wr_sem, os_sem, or_sem):
    me = lax.axis_index("pair")
    core = lax.axis_index("aux")
    z = me // PLANE
    g = me % PLANE
    x = g // SIDE
    y = g % SIDE
    base = z * PLANE
    up = ((z + 1) % PLANES) * PLANE + g
    down = ((z + PLANES - 1) % PLANES) * PLANE + g
    slot_base = base * BLK - HALO * BLK

    def moved(d):
        return ((x + d[0]) % SIDE) * SIDE + (y + d[1]) % SIDE

    def source(d):
        return ((x + SIDE - d[0]) % SIDE) * SIDE + (y + SIDE - d[1]) % SIDE

    loads = [pltpu.make_async_copy(a, b, load_sem.at[i]) for i, (a, b) in enumerate(
        ((pt_hbm, ptv), (slot_hbm, slotv), (v_hbm, vloc), (b_hbm, braw), (dom_hbm, domv)))]
    for copy in loads:
        copy.start()

    barrier = pltpu.get_barrier_semaphore()
    for d in ORDER:
        pl.semaphore_signal(barrier, inc=1, device_id=(base + moved(d), core), device_id_type=MESH)
    pl.semaphore_signal(barrier, inc=1, device_id=(up, core), device_id_type=MESH)
    pl.semaphore_signal(barrier, inc=1, device_id=(down, core), device_id_type=MESH)
    pl.semaphore_signal(barrier, inc=1, device_id=(me, 1 - core), device_id_type=MESH)

    load_pairs, load_slots, load_v, load_b, load_domains = loads
    load_pairs.wait()
    load_slots.wait()

    slot_row = slotv[...]
    blocks = slot_row.shape[1]
    pt = ptv[...]
    numbers = lax.broadcasted_iota(jnp.int32, (blocks, pt.shape[1]), 0)
    named_a = (numbers == pt[0:1]).astype(jnp.float32).astype(jnp.bfloat16)
    named_b = (numbers == pt[1:2]).astype(jnp.float32).astype(jnp.bfloat16)
    keep = (pt[0:1] != pt[1:2]).astype(jnp.float32)

    def pick(rows, first):
        wanted = lax.broadcasted_iota(jnp.int32, (rows, blocks), 0) + first
        return (wanted == slot_row).astype(jnp.float32).astype(jnp.bfloat16)

    pick_plane = pick(128, slot_base)
    pick_own = pick(16, (me - HALO // 2) * BLK)
    rows_a = dot(pick_own, named_a).astype(jnp.bfloat16)
    rows_b = (dot(pick_own, named_b) * keep).astype(jnp.bfloat16)
    cols_a = dot(pick_plane, named_a).astype(jnp.bfloat16)
    cols_b = dot(pick_plane, named_b).astype(jnp.bfloat16)
    counts = dot(rows_a, cols_b, ((1,), (1,))) + dot(rows_b, cols_a, ((1,), (1,)))
    load_v.wait()
    load_b.wait()
    marks = []
    for k in range(BLK):
        bf32[k] = braw[k].astype(jnp.float32)
        top = jnp.full((8, 128), 1e-30, jnp.float32)
        for p in range(AUXW):
            part = bf32[k, pl.ds(p, BS, stride=AUXW), :].astype(jnp.bfloat16)
            bt[k, :, p * BS:(p + 1) * BS] = part
            value = dot(part, vloc[k], ((0,), (0,)))
            yf32[p, k * BS:(k + 1) * BS, :] = value
            top = jnp.maximum(top, jnp.max(jnp.abs(value).reshape(BS // 8, 8, 128), axis=0))
        power = ceil_log2(jnp.max(top, axis=0, keepdims=True) * (1.0 / 32000.0))
        unit = jnp.exp2(-power)
        for p in range(AUXW):
            ysend[p, k * BS:(k + 1) * BS, :] = jnp.round(yf32[p, k * BS:(k + 1) * BS, :] * unit).astype(jnp.int16)
        marks.append(power)
    own_row = lax.broadcasted_iota(jnp.int32, (16, 128), 0)
    counts = jnp.where(own_row == OWN, marks[0], jnp.where(own_row == OWN + 1, marks[1], counts))
    cntsend[...] = counts.astype(jnp.bfloat16)
    cnt[g] = counts.astype(jnp.bfloat16)
    own_y = pltpu.make_async_copy(ysend.at[g], yraw.at[HALO + g], own_sem.at[0])
    own_y.start()

    pl.semaphore_wait(barrier, PLANE + 2)

    def count_copy(to, row):
        return pltpu.make_async_remote_copy(
            cntsend, cnt.at[row], cs_sem.at[to], cr_sem.at[row],
            device_id=(base + to, core), device_id_type=MESH)

    def y_copy(to, row):
        return pltpu.make_async_remote_copy(
            ysend.at[to], yraw.at[HALO + row], ys_sem.at[to], yr_sem.at[row],
            device_id=(base + to, core), device_id_type=MESH)

    def loop(lower, upper, body):
        def step(d, carry):
            body(d)
            return carry
        lax.fori_loop(lower, upper, step, 0)

    for d in ORDER:
        count_copy(moved(d), g).start()
    for d in ORDER:
        y_copy(moved(d), g).start()

    load_domains.wait()
    dom = domv[...]
    dom_high = (dom // 128).astype(jnp.float32).astype(jnp.bfloat16)
    dom_low = (dom % 128).astype(jnp.float32).astype(jnp.bfloat16)
    dom_win = dot(pick_plane, dom_high) * 128.0 + dot(pick_plane, dom_low)
    dom_t = dom_win.T
    for a in range(PLANE * BLK):
        column = dom_t[:, HALO * BLK + a:HALO * BLK + a + 1]
        domax[a] = jnp.broadcast_to(column, (128, 128)).astype(jnp.int32).astype(jnp.int16)
    for s in range(SLOTS):
        dombx[s] = jnp.broadcast_to(dom_win[s:s + 1], (16, 128)).astype(jnp.int32).astype(jnp.int16)

    for d in ORDER:
        count_copy(moved(d), source(d)).wait_recv()
    place_row = lax.broadcasted_iota(jnp.int32, (SLOTS, PLANE * 16), 0)
    place_col = lax.broadcasted_iota(jnp.int32, (SLOTS, PLANE * 16), 1)
    place_own = place_col % 16
    place = (place_row == BLK * (place_col // 16 + HALO // 2) + place_own) & (place_own < OWN)
    place_power = (place_row == BLK * (place_col // 16 + HALO) + place_own - OWN) & (place_own >= OWN) & (place_own < OWN + BLK)
    messages = cnt[...].reshape(PLANE * 16, 128)
    total = dot(place.astype(jnp.float32).astype(jnp.bfloat16), messages)
    power = dot(place_power.astype(jnp.float32).astype(jnp.bfloat16), messages)
    nsend[0] = jnp.concatenate([total[SLOTS - EDGE:], power[SLOTS - EDGE:SLOTS - EDGE // 2]], axis=0)
    nsend[1] = jnp.concatenate([total[:EDGE], power[EDGE // 2:EDGE]], axis=0)
    n_up = pltpu.make_async_remote_copy(nsend.at[0], nz.at[0], ns_sem.at[0], nr_sem.at[0],
                                        device_id=(up, core), device_id_type=MESH)
    n_down = pltpu.make_async_remote_copy(nsend.at[1], nz.at[1], ns_sem.at[1], nr_sem.at[1],
                                          device_id=(down, core), device_id_type=MESH)
    n_up.start()
    n_down.start()

    def spread(matrix):
        rows = matrix[HALO * BLK:HALO * BLK + PLANE * BLK]
        half = jnp.where(rows > 256.0, 0.5, 0.0)
        for n, side_of in enumerate((rows - half, rows + half)):
            for s in range(SLOTS):
                nx[n, s] = jnp.broadcast_to(side_of[:, s:s + 1], (PLANE * BLK, 128))

    def build(i):
        for k in range(BLK):
            a = i * BLK + k
            left = domax[a]
            for s in range(SPAN * BLK):
                weight = [jnp.broadcast_to(nx[n, i * BLK + s, pl.ds(a, 1), :], (16, 128)).astype(jnp.bfloat16)
                          for n in range(2)]
                right = dombx[i * BLK + s]
                for h in range(BS // 16):
                    tile = jnp.where(left[h * 16:(h + 1) * 16] == right, weight[h % 2], jnp.bfloat16(0))
                    mall[i, k * BS + h * 16:k * BS + (h + 1) * 16, s * BS:(s + 1) * BS] = tile

    spread(total)
    loop(HALO, PLANE - HALO, build)

    n_up.wait()
    n_down.wait()
    shift = PLANE * BLK
    lanes = lax.broadcasted_iota(jnp.int32, (EDGE, 128), 1)
    from_low = jnp.where(lanes < EDGE, pltpu.roll(nz[0, :EDGE], 128 - shift, 1), 0.0)
    from_high = jnp.where((lanes >= shift) & (lanes < SLOTS), pltpu.roll(nz[1, :EDGE], shift, 1), 0.0)
    total = total + jnp.concatenate([from_low, jnp.zeros((SLOTS - 2 * EDGE, 128), jnp.float32), from_high], axis=0)
    spread(total)
    power = jnp.concatenate([nz[0, EDGE:], power[EDGE // 2:SLOTS - EDGE // 2], nz[1, EDGE:]], axis=0)
    units = jnp.exp2(power)
    yunit[...] = units
    units = jnp.concatenate([units, jnp.zeros((128 - SLOTS, 128), jnp.float32)], axis=0).astype(jnp.bfloat16)
    bound = dot(total[HALO * BLK:HALO * BLK + PLANE * BLK].astype(jnp.bfloat16), units)
    wpower[...] = ceil_log2(jnp.maximum(bound, 1e-35) * 1.001)

    def z_copy(upward, n):
        row = (PLANE if upward else HALO) + n
        to = n if upward else HALO + PLANE + n
        side = 0 if upward else 1
        return pltpu.make_async_remote_copy(
            yraw.at[row], yraw.at[to],
            zs_sem.at[side, n], zr_sem.at[side, n],
            device_id=(up if upward else down, core), device_id_type=MESH)

    def relay(row):
        @pl.when(row >= PLANE - HALO)
        def _():
            z_copy(True, row - (PLANE - HALO)).start()

        @pl.when(row < HALO)
        def _():
            z_copy(False, row).start()

    def unpack(w):
        for k in range(BLK):
            value = yraw[w, k * BS:(k + 1) * BS, :].astype(jnp.float32) * yunit[pl.ds(w * BLK + k, 1), :]
            yw[pl.ds(w * MSG + k * BS, BS), :] = halves(value)

    def step(t):
        code = sum(jnp.where(t == n, SIDE * d[0] + d[1], 0) for n, d in enumerate(ORDER))
        return code // SIDE, code % SIDE

    own_y.wait()
    relay(g)
    unpack(HALO + g)

    def arrive(t):
        row = source(step(t))
        y_copy(row, row).wait_recv()
        relay(row)
        unpack(HALO + row)

    loop(0, 5, arrive)
    loop(0, HALO, build)
    loop(PLANE - HALO, PLANE, build)
    loop(5, PLANE - 1, arrive)

    def w_copy(i, row):
        return pltpu.make_async_remote_copy(
            wsend.at[i], wr.at[row], ws_sem.at[i], wr_sem.at[row],
            device_id=(base + i, core), device_id_type=MESH)

    def apply_index(i):
        both = dot(mall[i], yw[pl.ds(i * MSG, DEPTH), :])
        for k in range(BLK):
            part = both[k * BS:(k + 1) * BS]
            unit = jnp.exp2(-wpower[pl.ds(i * BLK + k, 1), :])
            wsend[i, k * BS:(k + 1) * BS, :] = jnp.round((part[:, :128] + part[:, 128:]) * unit).astype(jnp.int16)

        @pl.when(i != g)
        def _():
            w_copy(i, g).start()

    side = x // 2

    def turn(t):
        return sum(jnp.where(t == n, TURNS[n], 0) for n in range(SIDE))

    def inner(t):
        row = 2 - side + (t // SIDE) * (2 * side - 1)
        apply_index(row * SIDE + (y + turn(t % SIDE)) % SIDE)

    def outer(t):
        row = 3 - 3 * side + (t // SIDE) * (6 * side - 3)
        apply_index(row * SIDE + (y + turn(t % SIDE)) % SIDE)

    loop(0, 2 * SIDE, inner)
    for n in range(HALO):
        z_copy(True, n).wait()
        z_copy(False, n).wait()
        unpack(n)
        unpack(HALO + PLANE + n)
    loop(0, 2 * SIDE, outer)

    def gather(row):
        for k in range(BLK):
            wfull[k, pl.ds(row * BS, BS), :] = halves(wr[row, k * BS:(k + 1) * BS, :].astype(jnp.float32))

    own_w = pltpu.make_async_copy(wsend.at[g], wr.at[g], own_sem.at[1])
    own_w.start()
    own_w.wait()
    gather(g)

    def collect(t, first):
        sender = first + t % 2
        row = sender * SIDE + (y + SIDE - turn(t // 2)) % SIDE

        @pl.when(row != g)
        def _():
            w_copy(row, row).wait_recv()
            gather(row)

    swaps = [pltpu.make_async_remote_copy(acc.at[k], other.at[k], os_sem.at[k], or_sem.at[k],
                                          device_id=(me, 1 - core), device_id_type=MESH) for k in range(BLK)]
    half = AUXW * BS // 2
    for n in range(2):
        first = 2 * ((side + 1 + n) % 2)
        loop(0, 2 * SIDE, lambda t: collect(t, first))
        depth = pl.ds(pl.multiple_of(first // 2 * half, half), half)
        for k in range(BLK):
            both = dot(bt[k, :, depth], wfull[k, depth, :])
            part = both[:, :128] + both[:, 128:]
            if n == 0:
                acc[k] = part
            else:
                acc[k] = (acc[k] + part) * jnp.exp2(wpower[pl.ds(g * BLK + k, 1), :])
                swaps[k].start()

    for d in ORDER:
        count_copy(moved(d), g).wait_send()
        y_copy(moved(d), g).wait_send()
        w_copy(moved(d), g).wait_send()
    for k in range(BLK):
        swaps[k].wait()
        out_ref[k] = acc[k] + other[k]


def local(half_transformed, trials, pair_table, block_slot, domains):
    blocks = half_transformed.shape[0]
    count = block_slot.shape[0]
    vmem = pl.BlockSpec(memory_space=pltpu.VMEM)
    hbm = pl.BlockSpec(memory_space=pl.ANY)
    bf, f32 = jnp.bfloat16, jnp.float32
    dma = pltpu.SemaphoreType.DMA
    scratch = [
        pltpu.VMEM((BLK, BS * AUXW, 128), bf),
        pltpu.VMEM((BLK, BS, 128), bf),
        pltpu.VMEM((2, pair_table.shape[0]), jnp.int32),
        pltpu.VMEM((1, count), jnp.int32),
        pltpu.VMEM((count, 128), jnp.int32),
        pltpu.VMEM((BLK, BS * AUXW, 128), f32),
        pltpu.VMEM((BLK, BS, AUXW * 128), bf),
        pltpu.VMEM((AUXW, MSG, 128), f32),
        pltpu.VMEM((AUXW, MSG, 128), jnp.int16),
        pltpu.VMEM((WIN, MSG, 128), jnp.int16),
        pltpu.VMEM((WIN * MSG, 256), bf),
        pltpu.VMEM((SLOTS, 128), f32),
        pltpu.VMEM((PLANE * BLK, 128), f32),
        pltpu.VMEM((16, 128), bf),
        pltpu.VMEM((PLANE, 16, 128), bf),
        pltpu.VMEM((2, EDGE + EDGE // 2, 128), f32),
        pltpu.VMEM((2, EDGE + EDGE // 2, 128), f32),
        pltpu.VMEM((2, SLOTS, PLANE * BLK, 128), f32),
        pltpu.VMEM((PLANE * BLK, 128, 128), jnp.int16),
        pltpu.VMEM((SLOTS, 16, 128), jnp.int16),
        pltpu.VMEM((PLANE, MSG, DEPTH), bf),
        pltpu.VMEM((PLANE, MSG, 128), jnp.int16),
        pltpu.VMEM((AUXW, MSG, 128), jnp.int16),
        pltpu.VMEM((BLK, AUXW * 128, 256), bf),
        pltpu.VMEM((BLK, BS, 128), f32),
        pltpu.VMEM((BLK, BS, 128), f32),
        dma((5,)), dma((2,)), dma((PLANE,)), dma((PLANE,)), dma((2,)), dma((2,)),
        dma((PLANE,)), dma((PLANE,)), dma((2, HALO)), dma((2, HALO)), dma((PLANE,)), dma((PLANE,)), dma((BLK,)), dma((BLK,)),
    ]
    return pl.pallas_call(
        kernel,
        out_shape=jax.ShapeDtypeStruct(trials.shape, f32),
        in_specs=[hbm] * 5,
        out_specs=vmem,
        scratch_shapes=scratch,
        compiler_params=pltpu.CompilerParams(collective_id=1, has_side_effects=True, vmem_limit_bytes=62 << 20),
        name="exchange",
    )(half_transformed.reshape(blocks, BS * AUXW, 128), trials, pair_table.T,
      block_slot.reshape(1, -1), domains)


def solution(mesh):
    return jax.shard_map(
        local,
        mesh=mesh,
        in_specs=(P("pair", None, "aux", None), P("pair", None, None), P("pair", None), P(), P()),
        out_specs=P("pair", None, None),
        check_vma=False,
    )
```

```python
import jax
import jax.numpy as jnp
from jax import lax
from jax.experimental import pallas as pl
from jax.experimental.pallas import tpu as pltpu
from jax.sharding import PartitionSpec as P

MESH = pl.DeviceIdType.MESH
BS = 128
BLK = 2
PLANE = 16
PLANES = 8
AUXW = 16
HALO = 4
SPAN = 2 * HALO + 1
WIN = PLANE + 2 * HALO
SLOTS = WIN * BLK
EDGE = 2 * HALO * BLK
SIDE = 4
MSG = BLK * BS
OWN = (HALO + 1) * BLK
DEPTH = SPAN * MSG
ORDER = ((2, 2), (1, 2), (2, 1), (2, 3), (3, 2), (0, 2), (1, 1), (1, 3),
         (2, 0), (3, 1), (3, 3), (0, 1), (0, 3), (1, 0), (3, 0))
TURNS = (1, 2, 3, 0)


def dot(a, b, dims=((1,), (0,))):
    return lax.dot_general(a, b, (dims, ((), ())), preferred_element_type=jnp.float32)


def ceil_log2(value):
    return jnp.ceil(jnp.log(value) * 1.4426950408889634)


def halves(value):
    high = value.astype(jnp.bfloat16)
    low = (value - high.astype(jnp.float32)).astype(jnp.bfloat16)
    return jnp.concatenate([high, low], axis=1)


def kernel(b_hbm, v_hbm, pt_hbm, slot_hbm, dom_hbm, out_ref,
           braw, vloc, ptv, slotv, domv, bf32, bt, yf32, ysend, yraw, yw, yunit, wpower, cntsend, cnt, nsend, nz, nx, domax, dombx, mall,
           wsend, wr, wfull, acc, other,
           load_sem, own_sem, cs_sem, cr_sem, ns_sem, nr_sem, ys_sem, yr_sem, zs_sem, zr_sem,
           ws_sem, wr_sem, os_sem, or_sem):
    me = lax.axis_index("pair")
    core = lax.axis_index("aux")
    z = me // PLANE
    g = me % PLANE
    x = g // SIDE
    y = g % SIDE
    base = z * PLANE
    up = ((z + 1) % PLANES) * PLANE + g
    down = ((z + PLANES - 1) % PLANES) * PLANE + g
    slot_base = base * BLK - HALO * BLK

    def moved(d):
        return ((x + d[0]) % SIDE) * SIDE + (y + d[1]) % SIDE

    def source(d):
        return ((x + SIDE - d[0]) % SIDE) * SIDE + (y + SIDE - d[1]) % SIDE

    loads = [pltpu.make_async_copy(a, b, load_sem.at[i]) for i, (a, b) in enumerate(
        ((pt_hbm, ptv), (slot_hbm, slotv), (v_hbm, vloc), (b_hbm, braw), (dom_hbm, domv)))]
    for copy in loads:
        copy.start()

    barrier = pltpu.get_barrier_semaphore()
    for d in ORDER:
        pl.semaphore_signal(barrier, inc=1, device_id=(base + moved(d), core), device_id_type=MESH)
    pl.semaphore_signal(barrier, inc=1, device_id=(up, core), device_id_type=MESH)
    pl.semaphore_signal(barrier, inc=1, device_id=(down, core), device_id_type=MESH)
    pl.semaphore_signal(barrier, inc=1, device_id=(me, 1 - core), device_id_type=MESH)

    load_pairs, load_slots, load_v, load_b, load_domains = loads
    load_pairs.wait()
    load_slots.wait()

    slot_row = slotv[...]
    blocks = slot_row.shape[1]
    pt = ptv[...]
    numbers = lax.broadcasted_iota(jnp.int32, (blocks, pt.shape[1]), 0)
    named_a = (numbers == pt[0:1]).astype(jnp.float32).astype(jnp.bfloat16)
    named_b = (numbers == pt[1:2]).astype(jnp.float32).astype(jnp.bfloat16)
    keep = (pt[0:1] != pt[1:2]).astype(jnp.float32)

    def pick(rows, first):
        wanted = lax.broadcasted_iota(jnp.int32, (rows, blocks), 0) + first
        return (wanted == slot_row).astype(jnp.float32).astype(jnp.bfloat16)

    pick_plane = pick(128, slot_base)
    pick_own = pick(16, (me - HALO // 2) * BLK)
    rows_a = dot(pick_own, named_a).astype(jnp.bfloat16)
    rows_b = (dot(pick_own, named_b) * keep).astype(jnp.bfloat16)
    cols_a = dot(pick_plane, named_a).astype(jnp.bfloat16)
    cols_b = dot(pick_plane, named_b).astype(jnp.bfloat16)
    counts = dot(rows_a, cols_b, ((1,), (1,))) + dot(rows_b, cols_a, ((1,), (1,)))
    load_v.wait()
    load_b.wait()
    marks = []
    for k in range(BLK):
        bf32[k] = braw[k].astype(jnp.float32)
        top = jnp.full((8, 128), 1e-30, jnp.float32)
        for p in range(AUXW):
            part = bf32[k, pl.ds(p, BS, stride=AUXW), :].astype(jnp.bfloat16)
            bt[k, :, p * BS:(p + 1) * BS] = part
            value = dot(part, vloc[k], ((0,), (0,)))
            yf32[p, k * BS:(k + 1) * BS, :] = value
            top = jnp.maximum(top, jnp.max(jnp.abs(value).reshape(BS // 8, 8, 128), axis=0))
        power = ceil_log2(jnp.max(top, axis=0, keepdims=True) * (1.0 / 32000.0))
        unit = jnp.exp2(-power)
        for p in range(AUXW):
            ysend[p, k * BS:(k + 1) * BS, :] = jnp.round(yf32[p, k * BS:(k + 1) * BS, :] * unit).astype(jnp.int16)
        marks.append(power)
    own_row = lax.broadcasted_iota(jnp.int32, (16, 128), 0)
    counts = jnp.where(own_row == OWN, marks[0], jnp.where(own_row == OWN + 1, marks[1], counts))
    cntsend[...] = counts.astype(jnp.bfloat16)
    cnt[g] = counts.astype(jnp.bfloat16)
    own_y = pltpu.make_async_copy(ysend.at[g], yraw.at[HALO + g], own_sem.at[0])
    own_y.start()

    pl.semaphore_wait(barrier, PLANE + 2)

    def count_copy(to, row):
        return pltpu.make_async_remote_copy(
            cntsend, cnt.at[row], cs_sem.at[to], cr_sem.at[row],
            device_id=(base + to, core), device_id_type=MESH)

    def y_copy(to, row):
        return pltpu.make_async_remote_copy(
            ysend.at[to], yraw.at[HALO + row], ys_sem.at[to], yr_sem.at[row],
            device_id=(base + to, core), device_id_type=MESH)

    def loop(lower, upper, body):
        def step(d, carry):
            body(d)
            return carry
        lax.fori_loop(lower, upper, step, 0)

    for d in ORDER:
        count_copy(moved(d), g).start()
    for d in ORDER:
        y_copy(moved(d), g).start()

    load_domains.wait()
    dom = domv[...]
    dom_high = (dom // 128).astype(jnp.float32).astype(jnp.bfloat16)
    dom_low = (dom % 128).astype(jnp.float32).astype(jnp.bfloat16)
    dom_win = dot(pick_plane, dom_high) * 128.0 + dot(pick_plane, dom_low)
    dom_t = dom_win.T
    for a in range(PLANE * BLK):
        column = dom_t[:, HALO * BLK + a:HALO * BLK + a + 1]
        domax[a] = jnp.broadcast_to(column, (128, 128)).astype(jnp.int32).astype(jnp.int16)
    for s in range(SLOTS):
        dombx[s] = jnp.broadcast_to(dom_win[s:s + 1], (16, 128)).astype(jnp.int32).astype(jnp.int16)

    for d in ORDER:
        count_copy(moved(d), source(d)).wait_recv()
    place_row = lax.broadcasted_iota(jnp.int32, (SLOTS, PLANE * 16), 0)
    place_col = lax.broadcasted_iota(jnp.int32, (SLOTS, PLANE * 16), 1)
    place_own = place_col % 16
    place = (place_row == BLK * (place_col // 16 + HALO // 2) + place_own) & (place_own < OWN)
    place_power = (place_row == BLK * (place_col // 16 + HALO) + place_own - OWN) & (place_own >= OWN) & (place_own < OWN + BLK)
    messages = cnt[...].reshape(PLANE * 16, 128)
    total = dot(place.astype(jnp.float32).astype(jnp.bfloat16), messages)
    power = dot(place_power.astype(jnp.float32).astype(jnp.bfloat16), messages)
    nsend[0] = jnp.concatenate([total[SLOTS - EDGE:], power[SLOTS - EDGE:SLOTS - EDGE // 2]], axis=0)
    nsend[1] = jnp.concatenate([total[:EDGE], power[EDGE // 2:EDGE]], axis=0)
    n_up = pltpu.make_async_remote_copy(nsend.at[0], nz.at[0], ns_sem.at[0], nr_sem.at[0],
                                        device_id=(up, core), device_id_type=MESH)
    n_down = pltpu.make_async_remote_copy(nsend.at[1], nz.at[1], ns_sem.at[1], nr_sem.at[1],
                                          device_id=(down, core), device_id_type=MESH)
    n_up.start()
    n_down.start()

    def spread(matrix):
        rows = matrix[HALO * BLK:HALO * BLK + PLANE * BLK]
        half = jnp.where(rows > 256.0, 0.5, 0.0)
        for n, side_of in enumerate((rows - half, rows + half)):
            for s in range(SLOTS):
                nx[n, s] = jnp.broadcast_to(side_of[:, s:s + 1], (PLANE * BLK, 128))

    def build(i):
        for k in range(BLK):
            a = i * BLK + k
            left = domax[a]
            for s in range(SPAN * BLK):
                weight = [jnp.broadcast_to(nx[n, i * BLK + s, pl.ds(a, 1), :], (16, 128)).astype(jnp.bfloat16)
                          for n in range(2)]
                right = dombx[i * BLK + s]
                for h in range(BS // 16):
                    tile = jnp.where(left[h * 16:(h + 1) * 16] == right, weight[h % 2], jnp.bfloat16(0))
                    mall[i, k * BS + h * 16:k * BS + (h + 1) * 16, s * BS:(s + 1) * BS] = tile

    spread(total)
    loop(HALO, PLANE - HALO, build)

    n_up.wait()
    n_down.wait()
    shift = PLANE * BLK
    lanes = lax.broadcasted_iota(jnp.int32, (EDGE, 128), 1)
    from_low = jnp.where(lanes < EDGE, pltpu.roll(nz[0, :EDGE], 128 - shift, 1), 0.0)
    from_high = jnp.where((lanes >= shift) & (lanes < SLOTS), pltpu.roll(nz[1, :EDGE], shift, 1), 0.0)
    total = total + jnp.concatenate([from_low, jnp.zeros((SLOTS - 2 * EDGE, 128), jnp.float32), from_high], axis=0)
    spread(total)
    power = jnp.concatenate([nz[0, EDGE:], power[EDGE // 2:SLOTS - EDGE // 2], nz[1, EDGE:]], axis=0)
    units = jnp.exp2(power)
    yunit[...] = units
    units = jnp.concatenate([units, jnp.zeros((128 - SLOTS, 128), jnp.float32)], axis=0).astype(jnp.bfloat16)
    bound = dot(total[HALO * BLK:HALO * BLK + PLANE * BLK].astype(jnp.bfloat16), units)
    wpower[...] = ceil_log2(jnp.maximum(bound, 1e-35) * 1.001)

    def z_copy(upward, n):
        row = (PLANE if upward else HALO) + n
        to = n if upward else HALO + PLANE + n
        side = 0 if upward else 1
        return pltpu.make_async_remote_copy(
            yraw.at[row], yraw.at[to],
            zs_sem.at[side, n], zr_sem.at[side, n],
            device_id=(up if upward else down, core), device_id_type=MESH)

    def relay(row):
        @pl.when(row >= PLANE - HALO)
        def _():
            z_copy(True, row - (PLANE - HALO)).start()

        @pl.when(row < HALO)
        def _():
            z_copy(False, row).start()

    def unpack(w):
        for k in range(BLK):
            value = yraw[w, k * BS:(k + 1) * BS, :].astype(jnp.float32) * yunit[pl.ds(w * BLK + k, 1), :]
            yw[pl.ds(w * MSG + k * BS, BS), :] = halves(value)

    def step(t):
        code = sum(jnp.where(t == n, SIDE * d[0] + d[1], 0) for n, d in enumerate(ORDER))
        return code // SIDE, code % SIDE

    own_y.wait()
    relay(g)
    unpack(HALO + g)

    def arrive(t):
        row = source(step(t))
        y_copy(row, row).wait_recv()
        relay(row)
        unpack(HALO + row)

    loop(0, 5, arrive)
    loop(0, HALO, build)
    loop(PLANE - HALO, PLANE, build)
    loop(5, PLANE - 1, arrive)

    def w_copy(i, row):
        return pltpu.make_async_remote_copy(
            wsend.at[i], wr.at[row], ws_sem.at[i], wr_sem.at[row],
            device_id=(base + i, core), device_id_type=MESH)

    def apply_index(i):
        both = dot(mall[i], yw[pl.ds(i * MSG, DEPTH), :])
        for k in range(BLK):
            part = both[k * BS:(k + 1) * BS]
            unit = jnp.exp2(-wpower[pl.ds(i * BLK + k, 1), :])
            wsend[i, k * BS:(k + 1) * BS, :] = jnp.round((part[:, :128] + part[:, 128:]) * unit).astype(jnp.int16)

        @pl.when(i != g)
        def _():
            w_copy(i, g).start()

    side = x // 2

    def turn(t):
        return sum(jnp.where(t == n, TURNS[n], 0) for n in range(SIDE))

    def inner(t):
        row = 2 - side + (t // SIDE) * (2 * side - 1)
        apply_index(row * SIDE + (y + turn(t % SIDE)) % SIDE)

    def outer(t):
        row = 3 - 3 * side + (t // SIDE) * (6 * side - 3)
        apply_index(row * SIDE + (y + turn(t % SIDE)) % SIDE)

    loop(0, 2 * SIDE, inner)
    for n in range(HALO):
        z_copy(True, n).wait()
        z_copy(False, n).wait()
        unpack(n)
        unpack(HALO + PLANE + n)
    loop(0, 2 * SIDE, outer)

    def gather(row):
        for k in range(BLK):
            wfull[k, pl.ds(row * BS, BS), :] = halves(wr[row, k * BS:(k + 1) * BS, :].astype(jnp.float32))

    own_w = pltpu.make_async_copy(wsend.at[g], wr.at[g], own_sem.at[1])
    own_w.start()
    own_w.wait()
    gather(g)

    def collect(t, first):
        sender = first + t % 2
        row = sender * SIDE + (y + SIDE - turn(t // 2)) % SIDE

        @pl.when(row != g)
        def _():
            w_copy(row, row).wait_recv()
            gather(row)

    half = AUXW * BS // 2
    for n in range(2):
        first = 2 * ((side + 1 + n) % 2)
        loop(0, 2 * SIDE, lambda t: collect(t, first))
        depth = pl.ds(pl.multiple_of(first // 2 * half, half), half)
        for k in range(BLK):
            both = dot(bt[k, :, depth], wfull[k, depth, :])
            part = both[:, :128] + both[:, 128:]
            acc[k] = part if n == 0 else acc[k] + part

    for k in range(BLK):
        acc[k] = acc[k] * jnp.exp2(wpower[pl.ds(g * BLK + k, 1), :])
    swap = pltpu.make_async_remote_copy(acc, other, os_sem, or_sem,
                                        device_id=(me, 1 - core), device_id_type=MESH)
    swap.start()

    for d in ORDER:
        count_copy(moved(d), g).wait_send()
        y_copy(moved(d), g).wait_send()
        w_copy(moved(d), g).wait_send()
    swap.wait()
    out_ref[...] = acc[...] + other[...]


def local(half_transformed, trials, pair_table, block_slot, domains):
    blocks = half_transformed.shape[0]
    count = block_slot.shape[0]
    vmem = pl.BlockSpec(memory_space=pltpu.VMEM)
    hbm = pl.BlockSpec(memory_space=pl.ANY)
    bf, f32 = jnp.bfloat16, jnp.float32
    dma = pltpu.SemaphoreType.DMA
    scratch = [
        pltpu.VMEM((BLK, BS * AUXW, 128), bf),
        pltpu.VMEM((BLK, BS, 128), bf),
        pltpu.VMEM((2, pair_table.shape[0]), jnp.int32),
        pltpu.VMEM((1, count), jnp.int32),
        pltpu.VMEM((count, 128), jnp.int32),
        pltpu.VMEM((BLK, BS * AUXW, 128), f32),
        pltpu.VMEM((BLK, BS, AUXW * 128), bf),
        pltpu.VMEM((AUXW, MSG, 128), f32),
        pltpu.VMEM((AUXW, MSG, 128), jnp.int16),
        pltpu.VMEM((WIN, MSG, 128), jnp.int16),
        pltpu.VMEM((WIN * MSG, 256), bf),
        pltpu.VMEM((SLOTS, 128), f32),
        pltpu.VMEM((PLANE * BLK, 128), f32),
        pltpu.VMEM((16, 128), bf),
        pltpu.VMEM((PLANE, 16, 128), bf),
        pltpu.VMEM((2, EDGE + EDGE // 2, 128), f32),
        pltpu.VMEM((2, EDGE + EDGE // 2, 128), f32),
        pltpu.VMEM((2, SLOTS, PLANE * BLK, 128), f32),
        pltpu.VMEM((PLANE * BLK, 128, 128), jnp.int16),
        pltpu.VMEM((SLOTS, 16, 128), jnp.int16),
        pltpu.VMEM((PLANE, MSG, DEPTH), bf),
        pltpu.VMEM((PLANE, MSG, 128), jnp.int16),
        pltpu.VMEM((AUXW, MSG, 128), jnp.int16),
        pltpu.VMEM((BLK, AUXW * 128, 256), bf),
        pltpu.VMEM((BLK, BS, 128), f32),
        pltpu.VMEM((BLK, BS, 128), f32),
        dma((5,)), dma((2,)), dma((PLANE,)), dma((PLANE,)), dma((2,)), dma((2,)),
        dma((PLANE,)), dma((PLANE,)), dma((2, HALO)), dma((2, HALO)), dma((PLANE,)), dma((PLANE,)), dma, dma,
    ]
    return pl.pallas_call(
        kernel,
        out_shape=jax.ShapeDtypeStruct(trials.shape, f32),
        in_specs=[hbm] * 5,
        out_specs=vmem,
        scratch_shapes=scratch,
        compiler_params=pltpu.CompilerParams(collective_id=1, has_side_effects=True, vmem_limit_bytes=62 << 20),
        name="exchange",
    )(half_transformed.reshape(blocks, BS * AUXW, 128), trials, pair_table.T,
      block_slot.reshape(1, -1), domains)


def solution(mesh):
    return jax.shard_map(
        local,
        mesh=mesh,
        in_specs=(P("pair", None, "aux", None), P("pair", None, None), P("pair", None), P(), P()),
        out_specs=P("pair", None, None),
        check_vma=False,
    )
```
